256 devices in a mesh: dp: 4 (over x), phase: 4 (over y), mp: 16 (over z, core).
Axes of the slice: x: 4, y: 4, z: 8, core: 2. Of those that a mesh axis runs over, the one named last changes fastest.
Arguments:
- prompt_rows: bfloat16 [4, 8, 24, 8192], P('dp', 'phase', None, 'mp'), may hold values from -6 to 6
- row_dest: int32 [4, 8, 24], P(None, 'phase'), may hold values from 0 to 95, as said below
- segment_ids: int32 [4, 4, 48], P('dp'), may hold values from 0 to 5, never falling along the last dimension, each value on 1 to 24 neighbouring positions
- owner: int32 [4, 8, 3, 1], P('dp', 'phase'), may hold values from 0 to 3; in each aligned block of 3 rows (0 to 2, 3 to 5, ..., all dimensions but the last counted through in order) at most 2 rows name the same one
- gain: float32 [4, 8192], P('phase'), may hold values from 0.1 to 1.9
- w_query: bfloat16 [4, 8192, 4096], P('phase', 'dp', 'mp')
- w_key: bfloat16 [4, 8192, 512], P('phase', 'dp', 'mp')
- w_value: bfloat16 [4, 8192, 512], P('phase', 'dp', 'mp'), may hold values from -0.0625 to 0.0625
- w_out: bfloat16 [4, 4096, 8192], P('phase', 'dp', 'mp'), may hold values from -0.09375 to 0.09375
Outputs:
- embeddings: bfloat16 [4, 8, 8, 8192], P('dp', 'phase', None, 'mp')
The draws below stay inside these ranges and needn't reach their ends.
Inputs may be any that keep to these rules, and one draw needn't show every extreme that they name: `row_dest`: for each half micro-batch t, the values g * 24 + j over all loaders and rows name every group g and slot j exactly once; one loader sends at most 6 rows of one half micro-batch to one group, and every loader sends exactly 6 rows to some group. `segment_ids`: in each micro-batch every prompt number from 0 to 5 appears, on consecutive slots, at most 24 slots each. Within one half micro-batch of one group at most 2 prompts have the same owner, and in some half micro-batch exactly 2 do.
All inputs are finite; a program needn't handle non-finite values.
Results may differ from the reference program's by a relative error of at most 0.015.
Values may be sent and summed in bfloat16 or wider, within the bound.
A program may use at most 64 MiB of HBM per device.

```python
import math
import jax
import jax.numpy as jnp
import numpy as np
from jax import lax

D = 8192
HD = 128
QH = 32
KVH = 4
MB = 48
HALF = 24
M = 4
HALVES = 8
SEGS = 6
PH = 3
RCAP = 2
N_DP = 4
N_PHASE = 4


def shared_projection(key):
    return jax.random.normal(key, (N_PHASE, D, KVH * HD), jnp.float32)


def draw_w_key(key, part):
    shared = shared_projection(key)
    return (shared * D ** (-0.5)).astype(jnp.bfloat16)


def draw_w_query(key, part):
    key = jax.random.fold_in(key, 5)
    fresh_draw = jax.random.normal(key, (N_PHASE, D, QH * HD), jnp.float32)
    return (fresh_draw * D ** (-0.5)).astype(jnp.bfloat16)


def draw_row_dest(key, part):
    key = jax.random.fold_in(key, 11)
    widest = HALF // min(N_DP, 4)
    remain = HALF - widest
    others = max(N_DP - 1, 1)
    offsets = jnp.arange(N_DP, dtype=jnp.int32)
    quotas = jnp.where(offsets == 0, widest, remain // others + (offsets - 1 < remain % others).astype(jnp.int32))
    bounds = jnp.cumsum(quotas)
    row_ids = jnp.arange(HALF, dtype=jnp.int32)
    offset_of = jnp.sum((row_ids[:, None] >= bounds[None, :]).astype(jnp.int32), axis=1)

    def one_half(half_key):
        keys_four = jax.random.split(half_key, 4)
        loader_perm = jax.random.permutation(keys_four[0], N_DP).astype(jnp.int32)
        group_perm = jax.random.permutation(keys_four[1], N_DP).astype(jnp.int32)
        dest_groups = group_perm[(offsets[:, None] + offset_of[None, :]) % N_DP]
        row_keys = jax.random.split(keys_four[2], N_DP)
        shuffled = jax.vmap(lambda row_key, groups_row: groups_row[jax.random.permutation(row_key, HALF)])(row_keys, dest_groups)
        by_loader = jnp.zeros_like(shuffled).at[loader_perm].set(shuffled)
        flat_groups = by_loader.reshape(-1)
        hits_table = (flat_groups[:, None] == offsets[None, :]).astype(jnp.int32)
        ranks = jnp.sum((jnp.cumsum(hits_table, axis=0) - hits_table) * hits_table, axis=1)
        slot_perms = jax.vmap(lambda slot_key: jax.random.permutation(slot_key, HALF))(jax.random.split(keys_four[3], N_DP)).astype(jnp.int32)
        slot_values = slot_perms[flat_groups, ranks]
        return (flat_groups * HALF + slot_values).reshape(N_DP, HALF)
    return jnp.transpose(jax.vmap(one_half)(jax.random.split(key, HALVES)), (1, 0, 2)).astype(jnp.int32)


def block_levels(key, shape, cuts, least, top_value):
    loudness = 1.0
    for axis_at, blocks in cuts:
        steps = jax.random.uniform(jax.random.fold_in(jax.random.fold_in(key, 6), axis_at), (blocks,), jnp.float32, least / len(cuts), top_value / len(cuts))
        loudness = loudness * jnp.repeat(jnp.exp(steps), shape[axis_at] // blocks).reshape((-1,) + (1,) * (len(shape) - 1 - axis_at))
    return loudness


def profile(amount, total, bound, lean):
    weights = [(1 << 20) // math.isqrt(standing ** lean) + 1 for standing in range(2, amount + 1)]
    surplus, given = total - bound - (amount - 1), [1] * (amount - 1)
    while surplus > 0:
        movable = [i for i in range(amount - 1) if given[i] < bound]
        mass, budget = sum([weights[i] for i in movable]), surplus
        for i in movable:
            addition = min(bound - given[i], max(1, budget * weights[i] // mass), surplus)
            given[i] = given[i] + addition
            surplus = surplus - addition
    return np.array([bound] + given)


def ragged_sizes(own_key, number_of, total, reach, slope):
    if number_of == 2:
        one = jax.random.randint(own_key, (), max(1, total - reach), min(reach, total - 1) + 1)
        return jnp.stack([one, total - one])
    tallies = jnp.asarray(profile(number_of, total, reach, slope), jnp.int32)
    pairs = (number_of - 1) // 2
    source_of, sink = tallies[1:1 + 2 * pairs:2], tallies[2:2 + 2 * pairs:2]
    slack = jnp.minimum(source_of - 1, reach - sink)
    passed = jax.random.randint(jax.random.fold_in(own_key, 1), (pairs,), 0, 1 << 20) % (slack + 1)
    tallies = tallies.at[1:1 + 2 * pairs:2].set(source_of - passed).at[2:2 + 2 * pairs:2].set(sink + passed)
    return tallies[jax.random.permutation(jax.random.fold_in(own_key, 2), number_of)]


def shared_out(stream_key, own, number, rows, number_of, top, most, lean):
    ranking = jax.random.permutation(stream_key, number_of)
    crowded, usual = portions_of(number_of, rows * top, most, lean, True), portions_of(number_of, rows * top, most, lean, False)
    places = jnp.arange(number_of)

    def named(sizes, rotation):
        used = int((sizes > 0).sum())
        fixed = max(1, used // 4)
        shifted = fixed + (places - fixed + rotation * (used - fixed)) % max(1, number_of - fixed)
        return jnp.zeros((number_of,), jnp.int32).at[ranking[jnp.where(places < fixed, places, shifted)]].set(jnp.asarray(sizes, jnp.int32))

    sizes = jnp.where(number % 4 == 0, named(crowded, number // 4), named(usual, number - number // 4 - 1))
    mixed = jax.random.permutation(jax.random.fold_in(own, 3), number_of)
    giver, receiver = mixed[0:number_of // 2 * 2:2], mixed[1:number_of // 2 * 2:2]
    slack = jnp.minimum(sizes[giver] - 1, most - sizes[receiver]) // 2
    slack = jnp.where((giver == ranking[0]) | (receiver == ranking[0]) | (sizes[receiver] == 0), 0, jnp.maximum(slack, 0))
    shifted = jax.random.randint(jax.random.fold_in(own, 4), (number_of // 2,), 0, 1 << 20) % (slack + 1)
    sizes = sizes.at[giver].add(-shifted).at[receiver].add(shifted)
    labels = jnp.searchsorted(jnp.cumsum(sizes), jnp.arange(rows * top), side="right").astype(jnp.int32)
    table = labels.reshape(top, rows).T
    table = table[jax.random.permutation(jax.random.fold_in(own, 1), rows)]
    rotation = jax.random.randint(jax.random.fold_in(own, 2), (rows, 1), 0, top)
    return jnp.take_along_axis(table, (jnp.arange(top)[None, :] + rotation) % top, axis=1)


def portions_of(number_of, total, most, skew, full):
    portions = [(1 << 20) // math.isqrt(grade ** skew) + 1 for grade in range(1, number_of + 1)]
    largest = most if full else min(most, max(-(-total // number_of), total * portions[0] // sum(portions)))
    least = 1 if total - largest >= number_of - 1 else 0
    given, spare = [largest] + [least] * (number_of - 1), total - largest - least * (number_of - 1)
    while spare > 0:
        movable = [i for i in range(1, number_of) if given[i] < largest] or [i for i in range(1, number_of) if given[i] < most]
        whole, remaining = sum([portions[i] for i in movable]), spare
        for i in movable:
            extra = min(most - given[i], max(1, remaining * portions[i] // whole), spare)
            given[i] = given[i] + extra
            spare = spare - extra
    return np.array(given)


def bell_draw(own_key, extent, width, limit, cuts=(), kind=jnp.bfloat16):
    level = block_levels(own_key, extent, cuts, -0.22, 0.18) if cuts else 1.0
    values = jax.random.normal(own_key, extent, jnp.float32) * width * level
    return jnp.minimum(jnp.maximum(values, -limit), limit).astype(kind)


def setup_inputs(seed: int = 0) -> dict:
    seeds = jax.random.split(jax.random.key(seed), 10)
    prompt_rows = bell_draw(seeds[0], (N_DP, HALVES, HALF, D), 1.0, 6.0, ((0, 4), (1, 4), (3, 16)))
    row_dest = draw_row_dest(jax.random.fold_in(seeds[9], 71), 0)
    segment_ids = jax.vmap(lambda own: jnp.searchsorted(jnp.cumsum(ragged_sizes(own, SEGS, MB, MB // 2, 2)), jnp.arange(MB), side="right"))(jax.random.split(seeds[2], N_DP * M)).reshape((N_DP, M, MB)).astype(jnp.int32)
    owner_keys = jax.random.split(jax.random.fold_in(seeds[3], 1), N_DP * HALVES * PH // PH)
    owner_turns = jax.random.permutation(jax.random.fold_in(seeds[3], 3), N_DP * HALVES * PH // PH)
    owner = jax.vmap(lambda own, number: shared_out(jax.random.fold_in(seeds[3], 2), own, number, PH, N_DP, 1, RCAP, 2))(owner_keys, owner_turns).reshape((N_DP, HALVES, PH, 1))
    gain = jnp.clip(1.0 + 0.18 * jax.random.normal(seeds[4], (N_PHASE, D), jnp.float32), 0.1, 1.9)
    w_query = draw_w_query(jax.random.fold_in(seeds[9], 71), 0)
    w_key = draw_w_key(jax.random.fold_in(seeds[9], 71), 0)
    w_value = bell_draw(seeds[7], (N_PHASE, D, KVH * HD), D ** -0.5, 0.0625, ((0, 4), (1, 4), (2, 16)))
    w_out = bell_draw(seeds[8], (N_PHASE, QH * HD, D), (QH * HD) ** -0.5, 0.09375, ((0, 4), (1, 4), (2, 16)))
    return {"prompt_rows": prompt_rows, "row_dest": row_dest, "segment_ids": segment_ids, "owner": owner, "gain": gain, "w_query": w_query, "w_key": w_key, "w_value": w_value, "w_out": w_out}


NORM_EPS = 1e-05

def pack_stream(prompt_rows, row_dest):
    flat_rows = prompt_rows.transpose(1, 0, 2, 3).reshape(HALVES, N_DP * HALF, D)
    flat_dest = row_dest.transpose(1, 0, 2).reshape(HALVES, N_DP * HALF).astype(jnp.int32)
    half_ids = jnp.broadcast_to(jnp.arange(HALVES, dtype=jnp.int32)[:, None], flat_dest.shape)
    packed = jnp.zeros((HALVES, N_DP * HALF, D), jnp.bfloat16).at[half_ids, flat_dest].set(flat_rows)
    packed = packed.reshape(HALVES, N_DP, HALF, D).transpose(1, 0, 2, 3)
    return packed.reshape(N_DP * M, MB, D)

def attend_batch(qkv_rows, segments):
    query_width = QH * HD
    pair_width = KVH * HD
    query_rows = qkv_rows[:, :query_width].astype(jnp.float32).reshape(MB, QH, HD)
    key_rows = qkv_rows[:, query_width:query_width + pair_width].astype(jnp.float32).reshape(MB, KVH, HD)
    value_rows = qkv_rows[:, query_width + pair_width:].astype(jnp.float32).reshape(MB, KVH, HD)
    key_rows = jnp.repeat(key_rows, QH // KVH, axis=1)
    value_rows = jnp.repeat(value_rows, QH // KVH, axis=1)
    scores = jnp.einsum('qhd,khd->hqk', query_rows, key_rows) * HD ** (-0.5)
    places = jnp.arange(MB, dtype=jnp.int32)
    allowed = (segments[:, None] == segments[None, :]) & (places[None, :] <= places[:, None])
    scores = jnp.where(allowed[None, :, :], scores, -jnp.inf)
    row_top = lax.optimization_barrier(jnp.max(scores, axis=2, keepdims=True))
    weights = jnp.exp(scores - row_top)
    probabilities = (weights / lax.optimization_barrier(jnp.sum(weights, axis=2, keepdims=True))).astype(jnp.bfloat16)
    mixed = jnp.einsum('hqk,khd->qhd', probabilities.astype(jnp.float32), value_rows)
    return mixed.astype(jnp.bfloat16).reshape(MB, QH * HD)

def apply_layer(hidden, gain_row, w_qkv, w_back, segments):
    tok_float = hidden.astype(jnp.float32).reshape(-1, D)
    squares = lax.optimization_barrier(jnp.sum(tok_float * tok_float, axis=1))
    gated = (tok_float * gain_row[None, :]).astype(jnp.bfloat16)
    qkv_sums = jnp.dot(gated, w_qkv, preferred_element_type=jnp.float32)
    qkv_rows = (qkv_sums * lax.rsqrt(squares / D + NORM_EPS)[:, None]).astype(jnp.bfloat16)
    mixed = jax.vmap(attend_batch)(qkv_rows.reshape(-1, MB, (QH + 2 * KVH) * HD), segments)
    updated = tok_float + jnp.dot(mixed.reshape(-1, QH * HD), w_back, preferred_element_type=jnp.float32)
    return updated.astype(jnp.bfloat16).reshape(hidden.shape)

def reference(prompt_rows, row_dest, segment_ids, owner, gain, w_query, w_key, w_value, w_out):
    hidden = pack_stream(prompt_rows, row_dest)
    segments = segment_ids.reshape(N_DP * M, MB).astype(jnp.int32)
    for section in range(N_PHASE):
        w_qkv = jnp.concatenate([w_query[section], w_key[section], w_value[section]], axis=1)
        hidden = apply_layer(hidden, gain[section], w_qkv, w_out[section], segments)
    segment_hits = (segments[:, None, :] == jnp.arange(SEGS, dtype=jnp.int32)[None, :, None]).astype(jnp.float32)
    segment_sums = jnp.einsum('bsn,bnd->bsd', segment_hits, hidden.astype(jnp.float32))
    counts = lax.optimization_barrier(jnp.sum(segment_hits, axis=2))
    pooled = (segment_sums / counts[:, :, None]).astype(jnp.bfloat16).reshape(N_DP, HALVES, PH, D)
    owner_ids = owner[..., 0].astype(jnp.int32)
    hits_table = (owner_ids[..., None] == jnp.arange(N_DP, dtype=jnp.int32)).astype(jnp.int32)
    ranks = lax.optimization_barrier(jnp.sum((jnp.cumsum(hits_table, axis=2) - hits_table) * hits_table, axis=-1))
    columns = jnp.arange(N_DP, dtype=jnp.int32)[:, None, None] * RCAP + ranks
    half_ids = jnp.broadcast_to(jnp.arange(HALVES, dtype=jnp.int32)[None, :, None], owner_ids.shape)
    result = jnp.zeros((N_DP, HALVES, N_DP * RCAP, D), jnp.bfloat16)
    return result.at[owner_ids, half_ids, columns].set(pooled)
```

```python
import jax
import jax.numpy as jnp
from jax import lax
from jax.experimental import pallas as pl
from jax.experimental.pallas import tpu as pltpu
from jax.sharding import PartitionSpec as P

MESH = pl.DeviceIdType.MESH
F32 = jnp.float32
BF16 = jnp.bfloat16
I32 = jnp.int32

D = 8192
HD = 128
MB = 48
M = 4
NX = 4
NZ = 8
EPS = 1e-05
BLK = 512


def iota(shape, dim):
    return lax.broadcasted_iota(I32, shape, dim)


def dot(a, b):
    return jnp.dot(a, b, preferred_element_type=F32)


def dot_nt(a, b):
    return lax.dot_general(a, b, (((1,), (1,)), ((), ())), preferred_element_type=F32)


def to_row(col):
    eye = iota((MB, 128), 0) == iota((MB, 128), 1)
    return jnp.sum(jnp.where(eye, col, 0.0), axis=0, keepdims=True)


def to_col(row):
    eye = iota((MB, MB), 0) == iota((MB, MB), 1)
    return jnp.sum(jnp.where(eye, row, 0.0), axis=1, keepdims=True)


def kernel(
    rows, row_dest, segs, owner, gain, wq, wk, wv, wo, out,
    raw, seg, code, wq_v, wk_v, wv_v, kvt, wkv_v, wo_v,
    hid, q_out, q_in, s_out, s_in, mx, mixed, o_out, o_in, h_out, e_out, e_in,
    loc, one_s, one_r, x3_s, x3_r, kv_s, kv_r, pro_s, h_r,
    q_s, q_r, s_s, s_r, mx_s, mx_r, o_s, o_r, h_s, e_s, e_r,
):
    x = lax.axis_index("dp")
    y = lax.axis_index("phase")
    p = lax.axis_index("mp")
    z = p // 2
    c = p % 2
    ring = z // 2
    odd = z % 2

    def at(xx, yy, zz, cc):
        return (xx, yy, zz * 2 + cc)

    def remote(src, dst, send, recv, device):
        return pltpu.make_async_remote_copy(
            src_ref=src, dst_ref=dst, send_sem=send, recv_sem=recv,
            device_id=device, device_id_type=MESH,
        )

    def local(src, dst, sem):
        return pltpu.make_async_copy(src, dst, sem)

    def settle(ref, sem):
        pltpu.make_async_copy(ref, ref, sem).wait()

    def turn(k):
        return (x + k) % NX

    loads = [
        local(rows, raw.at[x], loc.at[0]),
        local(wk, wk_v, loc.at[1]),
        local(wv, wv_v, loc.at[2]),
        local(wq, wq_v.at[c], loc.at[3]),
        local(wo, wo_v.at[c], loc.at[4]),
    ]
    for load in loads:
        load.start()

    barrier = pltpu.get_barrier_semaphore()

    def greet(device):
        pl.semaphore_signal(barrier, inc=1, device_id=device, device_id_type=MESH)

    pair_z = z + 1 - 2 * odd
    self_mx = x == ring
    self_pro = (y == 0) & (x == ring) & (c == x // 2)
    self_e = (y == 3) & (x % 2 == c)
    greet(at(x, y, z, 1 - c))
    greet(at(x, y, pair_z, 0))
    greet(at(x, y, pair_z, 1))
    for k in range(1, NX):
        greet(at(turn(k), y, z, c))
    for r in range(NX):
        for e in range(2):
            @pl.when(jnp.logical_not((x == r) & (2 * x + e == z)))
            def _():
                greet(at(r, y, 2 * x + e, c))

    @pl.when(y > 0)
    def _():
        for r in range(NX):
            for e in range(2):
                greet(at(r, y - 1, 2 * x + e, c))

    @pl.when(y == 0)
    def _():
        for f in range(M):
            for gg in range(2):
                for e in range(2):
                    for cc in range(2):
                        if f == 0:
                            @pl.when(jnp.logical_not((2 * c + gg == x) & (2 * x + e == z) & (c == cc)))
                            def _():
                                greet(at(2 * c + gg, f, 2 * x + e, cc))
                        else:
                            greet(at(2 * c + gg, f, 2 * x + e, cc))

    for b in range(2):
        for cc in range(2):
            @pl.when(jnp.logical_not((y == 3) & (c + 2 * b == x) & (c == cc)))
            def _():
                greet(at(c + 2 * b, 3, z, cc))

    seg[x] = jnp.zeros((8, 128), I32)
    seg[x, 0:4, 0:MB] = segs[0]
    lane = iota((8, 128), 1)
    table = jnp.full((8, 128), -1, I32)
    for t in range(2):
        for i in range(3):
            who = owner[t, i]
            rank = jnp.int32(0)
            for before in range(i):
                rank = rank + (owner[t, before] == who).astype(I32)
            table = jnp.where(lane == 3 * t + i, 2 * who + rank, table)
    code[x] = table

    count = 22 - self_mx.astype(I32) - self_pro.astype(I32)
    count = count + jnp.where(y < 3, 8, 16) - self_e.astype(I32)
    pl.semaphore_wait(barrier, count)

    loads[0].wait()
    for k in range(1, NX):
        remote(raw.at[x], raw.at[x], x3_s.at[0], x3_r.at[0], at(turn(k), y, z, c)).start()
    for k in range(1, NX):
        remote(seg.at[x], seg.at[x], x3_s.at[1], x3_r.at[1], at(turn(k), y, z, c)).start()
        remote(code.at[x], code.at[x], x3_s.at[2], x3_r.at[2], at(turn(k), y, z, c)).start()
    loads[3].wait()
    remote(wq_v.at[c], wq_v.at[c], one_s.at[0], one_r.at[0], at(x, y, z, 1 - c)).start()
    loads[4].wait()
    remote(wo_v.at[c], wo_v.at[c], one_s.at[1], one_r.at[1], at(x, y, z, 1 - c)).start()

    loads[1].wait()
    loads[2].wait()
    quad = 2 * odd + c
    kvt[quad, 0] = wk_v[...].T
    kvt[quad, 1] = wv_v[...].T
    mine = kvt.at[quad]
    remote(mine, mine, kv_s, kv_r, at(x, y, z, 1 - c)).start()
    remote(mine, mine, kv_s, kv_r, at(x, y, pair_z, 0)).start()
    remote(mine, mine, kv_s, kv_r, at(x, y, pair_z, 1)).start()

    settle(raw.at[0:3], x3_r.at[0])
    dest = row_dest[...].astype(F32)
    spread = [
        (iota((24, MB), 0) + 24 * t == iota((24, MB), 1)).astype(F32) for t in range(2)
    ]
    dest = dot(dest[:, 0, :], spread[0]) + dot(dest[:, 1, :], spread[1])
    slot = iota((MB, MB), 0)
    place = iota((MB, MB), 1)
    upper = slot >= 24
    wanted = (slot - jnp.where(upper, 24, 0) + 24 * x).astype(F32)
    same_half = upper == (place >= 24)
    packed = jnp.zeros((MB, BLK), F32)
    for l in range(NX):
        hits = same_half & (dest[l : l + 1, :] == wanted)
        packed = packed + dot(hits.astype(BF16), raw[l])
    h_out[y] = packed.astype(BF16)
    first = hid.at[y, (x % 2) * 4 + quad]

    @pl.when(self_pro)
    def _():
        local(h_out.at[y], first, h_r.at[y]).start()

    @pl.when(jnp.logical_not(self_pro))
    def _():
        remote(h_out.at[y], first, pro_s.at[0], h_r.at[y], at(ring, 0, z, x // 2)).start()

    for dz in range(1, NZ):
        remote(
            h_out.at[y], first, pro_s.at[1], h_r.at[y], at(ring, 0, (z + dz) % NZ, x // 2)
        ).start()

    settle(kvt.at[0:3], kv_r)
    for t in range(2):
        wkv_v[:, 128 * t : 128 * t + 128] = jnp.concatenate(
            [kvt[j, t] for j in range(4)], axis=0
        ).T
    settle(wq_v.at[0], one_r.at[0])
    settle(wo_v.at[0], one_r.at[1])
    settle(seg.at[0:3], x3_r.at[1])
    settle(code.at[0:3], x3_r.at[2])

    group = 2 * c + x // 2
    block = (x // 2) * 4 + 2 * odd + x % 2

    def project(m):
        settle(hid.at[m], h_r.at[m])
        squares = jnp.zeros((2 * MB, 128), F32)
        sums = [jnp.zeros((2 * MB, 256), F32) for _ in range(3)]
        for j in range(4):
            h = jnp.concatenate([hid[m, j], hid[m, 4 + j]], axis=0).astype(F32)
            square = h * h
            for i in range(4):
                squares = squares + square[:, 128 * i : 128 * i + 128]
            g = gain[:, pl.ds(pl.multiple_of(x * 2048 + BLK * j, BLK), BLK)]
            gated = (h * g).astype(BF16)
            ks = slice(BLK * j, BLK * j + BLK)
            sums[0] = sums[0] + dot(gated, wq_v[0, ks])
            sums[1] = sums[1] + dot(gated, wq_v[1, ks])
            sums[2] = sums[2] + dot(gated, wkv_v[ks])
        total = jnp.sum(squares, axis=1, keepdims=True)
        for gg in range(2):
            part = slice(MB * gg, MB * gg + MB)
            s_out[m, gg] = jnp.broadcast_to(to_row(total[part]), (8, 128))
            for jj in range(2):
                q_out[m, 2 * gg + jj, :, 0:256] = sums[jj][part].astype(BF16)
                q_out[m, 2 * gg + jj, :, 256:512] = sums[2][part].astype(BF16)
        for k in range(1, NX):
            to = turn(k)
            remote(
                q_out.at[m, to], q_in.at[m, k - 1], q_s.at[m], q_r.at[m], at(to, y, z, c)
            ).start()
            remote(
                s_out.at[m, to // 2], s_in.at[m, k - 1], s_s.at[m], s_r.at[m], at(to, y, z, c)
            ).start()

    def attend(m):
        settle(s_in.at[m], s_r.at[m])
        settle(q_in.at[m], q_r.at[m])
        squares = s_out[m, x // 2] + s_in[m, 0] + s_in[m, 1] + s_in[m, 2]
        scale = lax.rsqrt(to_col(squares[0:1, 0:MB]) / D + EPS)
        qkv = q_out[m, x].astype(F32)
        for k in range(3):
            qkv = qkv + q_in[m, k].astype(F32)
        qkv = (qkv * scale).astype(BF16)
        query = jnp.concatenate([qkv[:, 0:128], qkv[:, 128:256]], axis=0)
        scores = dot_nt(query, qkv[:, 256:384]) * HD ** (-0.5)
        seg_row = seg[group, pl.ds(m, 1), :][:, 0:MB].astype(F32)
        allowed = (to_col(seg_row) == seg_row) & (iota((MB, MB), 1) <= iota((MB, MB), 0))
        top, low = scores[:MB], scores[MB:]
        halves = []
        for part in (top, low):
            part = jnp.where(allowed, part, -jnp.inf)
            weights = jnp.exp(part - jnp.max(part, axis=1, keepdims=True))
            halves.append((weights / jnp.sum(weights, axis=1, keepdims=True)).astype(BF16))
        for i in range(2):
            mx[m, :, 128 * i : 128 * i + 128] = dot(halves[i], qkv[:, 384:512]).astype(BF16)
        for dz in range(NZ):
            zz = (z + dz) % NZ
            if dz == 0:
                @pl.when(self_mx)
                def _():
                    local(mx.at[m], mixed.at[m, block], mx_r.at[m]).start()

                @pl.when(jnp.logical_not(self_mx))
                def _():
                    remote(
                        mx.at[m], mixed.at[m, block], mx_s.at[0, m], mx_r.at[m], at(ring, y, zz, c)
                    ).start()
            else:
                remote(
                    mx.at[m], mixed.at[m, block], mx_s.at[1, m], mx_r.at[m], at(ring, y, zz, c)
                ).start()

    def back(m):
        settle(mixed.at[m], mx_r.at[m])
        whole = [jnp.concatenate([mixed[m, j], mixed[m, 4 + j]], axis=0) for j in range(4)]
        for jj in range(2):
            sums = jnp.zeros((2 * MB, BLK), F32)
            for j in range(4):
                sums = sums + dot(whole[j], wo_v[jj, 256 * j : 256 * j + 256])
            for gg in range(2):
                kept = hid[m, 4 * gg + 2 * odd + jj].astype(F32)
                kept = jnp.where(x == ring, kept, 0.0)
                o_out[m, 2 * gg + jj] = (sums[MB * gg : MB * gg + MB] + kept).astype(BF16)
        for k in range(1, NX):
            to = turn(k)
            remote(
                o_out.at[m, to], o_in.at[m, k - 1], o_s.at[m], o_r.at[m], at(to, y, z, c)
            ).start()

    def forward(m):
        settle(o_in.at[m], o_r.at[m])
        new = o_out[m, x].astype(F32)
        for k in range(3):
            new = new + o_in[m, k].astype(F32)
        new = new.astype(BF16)

        @pl.when(y < 3)
        def _():
            h_out[M + m] = new
            for dz in range(NZ):
                remote(
                    h_out.at[M + m], hid.at[m, block], h_s.at[m], h_r.at[m],
                    at(ring, y + 1, (z + dz) % NZ, c),
                ).start()

        @pl.when(y == 3)
        def _():
            seg_row = seg[group, pl.ds(m, 1), :][:, 0:MB]
            hits = seg_row == iota((16, MB), 0)
            amount = jnp.maximum(jnp.sum(hits.astype(F32), axis=1, keepdims=True), 1.0)
            e_out[m] = (dot(hits.astype(BF16), new) / amount).astype(BF16)
            for k in range(NX):
                to = at(turn(k), m, z, x % 2)
                if k == 0:
                    is_self = (m == 3) & (x % 2 == c)

                    @pl.when(is_self)
                    def _():
                        local(e_out.at[m], e_in.at[group], e_r).start()

                    @pl.when(jnp.logical_not(is_self))
                    def _():
                        remote(e_out.at[m], e_in.at[group], e_s.at[0, m], e_r, to).start()
                else:
                    remote(e_out.at[m], e_in.at[group], e_s.at[1, m], e_r, to).start()

    def tick(i, carry):
        @pl.when(i < M)
        def _():
            project(i)

        @pl.when(i > 0)
        def _():
            back(i - 1)

        @pl.when(i < M)
        def _():
            attend(i)

        @pl.when(i > 0)
        def _():
            forward(i - 1)

        return carry

    lax.fori_loop(0, M + 1, tick, 0)

    settle(raw.at[0:3], x3_s.at[0])
    settle(seg.at[0:3], x3_s.at[1])
    settle(code.at[0:3], x3_s.at[2])
    settle(wq_v.at[0], one_s.at[0])
    settle(wo_v.at[0], one_s.at[1])
    settle(kvt.at[0:3], kv_s)

    @pl.when(jnp.logical_not(self_pro))
    def _():
        settle(h_out.at[0], pro_s.at[0])

    settle(hid.at[0, 0:7], pro_s.at[1])

    def drain(m, carry):
        settle(q_in.at[m], q_s.at[m])
        settle(s_in.at[m], s_s.at[m])
        settle(o_in.at[m], o_s.at[m])
        settle(mixed.at[m, 0:7], mx_s.at[1, m])

        @pl.when(jnp.logical_not(self_mx))
        def _():
            settle(mx.at[m], mx_s.at[0, m])

        @pl.when(y < 3)
        def _():
            settle(hid.at[m], h_s.at[m])

        @pl.when(y == 3)
        def _():
            settle(e_in.at[0:3], e_s.at[1, m])

            @pl.when(jnp.logical_not((m == 3) & (x % 2 == c)))
            def _():
                settle(e_in.at[0], e_s.at[0, m])

        return carry

    lax.fori_loop(0, M, drain, 0)

    settle(e_in, e_r)
    row = iota((16, 16), 0)
    col = iota((16, 16), 1)
    picked = jnp.zeros((16, BLK), F32)
    for g in range(NX):
        hits = ((row >> 1) & 3) == g
        hits = hits & ((row >= 8) == (col >= 3)) & (col < 6)
        hits = hits & (code[g, 0:1, 0:16] == 2 * x + (row & 1))
        picked = picked + dot(hits.astype(BF16), e_in[g])
    out[...] = picked.astype(BF16)


def shards(prompt_rows, row_dest, segment_ids, owner, gain, w_query, w_key, w_value, w_out):
    any_spec = pl.BlockSpec(memory_space=pl.ANY)
    vmem = pl.BlockSpec(memory_space=pltpu.VMEM)
    smem = pl.BlockSpec(memory_space=pltpu.SMEM)
    dma = pltpu.SemaphoreType.DMA
    embedded = pl.pallas_call(
        kernel,
        out_shape=jax.ShapeDtypeStruct((16, BLK), BF16),
        in_specs=[any_spec, vmem, vmem, smem, vmem, any_spec, any_spec, any_spec, any_spec],
        out_specs=vmem,
        scratch_shapes=[
            pltpu.VMEM((NX, MB, BLK), BF16),
            pltpu.VMEM((NX, 8, 128), I32),
            pltpu.VMEM((NX, 8, 128), I32),
            pltpu.VMEM((2, 2048, 256), BF16),
            pltpu.VMEM((2048, 32), BF16),
            pltpu.VMEM((2048, 32), BF16),
            pltpu.VMEM((4, 2, 32, 2048), BF16),
            pltpu.VMEM((2048, 256), BF16),
            pltpu.VMEM((2, 1024, BLK), BF16),
            pltpu.VMEM((M, 8, MB, BLK), BF16),
            pltpu.VMEM((M, 4, MB, BLK), BF16),
            pltpu.VMEM((M, 3, MB, BLK), BF16),
            pltpu.VMEM((M, 2, 8, 128), F32),
            pltpu.VMEM((M, 3, 8, 128), F32),
            pltpu.VMEM((M, MB, 256), BF16),
            pltpu.VMEM((M, 8, MB, 256), BF16),
            pltpu.VMEM((M, 4, MB, BLK), BF16),
            pltpu.VMEM((M, 3, MB, BLK), BF16),
            pltpu.VMEM((2 * M, MB, BLK), BF16),
            pltpu.VMEM((M, 16, BLK), BF16),
            pltpu.VMEM((NX, 16, BLK), BF16),
            dma((5,)),
            dma((2,)),
            dma((2,)),
            dma((3,)),
            dma((3,)),
            dma,
            dma,
            dma((2,)),
            dma((M,)),
            dma((M,)),
            dma((M,)),
            dma((M,)),
            dma((M,)),
            dma((2, M)),
            dma((M,)),
            dma((M,)),
            dma((M,)),
            dma((M,)),
            dma((2, M)),
            dma,
        ],
        compiler_params=pltpu.CompilerParams(
            collective_id=0, has_side_effects=True, vmem_limit_bytes=48 << 20
        ),
        name="sections",
    )(
        prompt_rows.reshape(MB, BLK),
        row_dest,
        segment_ids,
        owner.reshape(2, 3),
        gain,
        w_query[0],
        w_key[0],
        w_value[0],
        w_out[0],
    )
    return embedded.reshape(1, 2, 8, BLK)


def solution(mesh):
    in_specs = (
        P("dp", "phase", None, "mp"),
        P(None, "phase", None),
        P("dp", None, None),
        P("dp", "phase", None, None),
        P("phase", None),
        P("phase", "dp", "mp"),
        P("phase", "dp", "mp"),
        P("phase", "dp", "mp"),
        P("phase", "dp", "mp"),
    )
    out_specs = P("dp", "phase", None, "mp")
    return jax.shard_map(shards, mesh=mesh, in_specs=in_specs, out_specs=out_specs, check_vma=False)
```

```python
import jax
import jax.numpy as jnp
from jax import lax
from jax.experimental import pallas as pl
from jax.experimental.pallas import tpu as pltpu
from jax.sharding import PartitionSpec as P

MESH = pl.DeviceIdType.MESH
F32 = jnp.float32
BF16 = jnp.bfloat16
I32 = jnp.int32

D = 8192
HD = 128
MB = 48
M = 4
NX = 4
NZ = 8
EPS = 1e-05
BLK = 512
T = 2 * M
FAR = (4, 3, 5, 2, 6, 1, 7)


def iota(shape, dim):
    return lax.broadcasted_iota(I32, shape, dim)


def dot(a, b):
    return jnp.dot(a, b, preferred_element_type=F32)


def dot_nt(a, b):
    return lax.dot_general(a, b, (((1,), (1,)), ((), ())), preferred_element_type=F32)


def to_row(col):
    eye = iota((MB, 128), 0) == iota((MB, 128), 1)
    return jnp.sum(jnp.where(eye, col, 0.0), axis=0, keepdims=True)


def to_col(row):
    eye = iota((MB, MB), 0) == iota((MB, MB), 1)
    return jnp.sum(jnp.where(eye, row, 0.0), axis=1, keepdims=True)


def kernel(
    rows, row_dest, segs, owner, gain, wq, wk, wv, wo, out,
    raw, seg, code, wq_v, kvt, wkv_v, wo_v, packed,
    hid, q_out, q_in, s_out, s_in, mx, mixed, o_out, o_in, h_out, e_out, e_in,
    loc, one_s, one_r, x3_s, x3_r, kv_s, kv_r, pro_s, h_r,
    q_s, q_r, s_s, s_r, mx_s, mx_r, o_s, o_r, h_s, e_s, e_r, go,
):
    x = lax.axis_index("dp")
    y = lax.axis_index("phase")
    p = lax.axis_index("mp")
    z = p // 2
    c = p % 2
    ring = z // 2
    odd = z % 2

    def at(xx, yy, zz, cc):
        return (xx, yy, zz * 2 + cc)

    def remote(src, dst, send, recv, device):
        return pltpu.make_async_remote_copy(
            src_ref=src, dst_ref=dst, send_sem=send, recv_sem=recv,
            device_id=device, device_id_type=MESH,
        )

    def local(src, dst, sem):
        return pltpu.make_async_copy(src, dst, sem)

    def settle(ref, sem):
        pltpu.make_async_copy(ref, ref, sem).wait()

    def turn(k):
        return (x + k) % NX

    quad = 2 * odd + c
    loads = [
        local(rows, raw.at[x], loc.at[0]),
        local(wk, kvt.at[quad, 0], loc.at[1]),
        local(wv, kvt.at[quad, 1], loc.at[2]),
        local(wq, wq_v.at[c], loc.at[3]),
        local(wo, wo_v.at[c], loc.at[4]),
    ]
    for load in loads:
        load.start()

    barrier = pltpu.get_barrier_semaphore()

    def greet(device):
        pl.semaphore_signal(barrier, inc=1, device_id=device, device_id_type=MESH)

    pair_z = z + 1 - 2 * odd
    self_mx = x == ring
    self_pro = (y == 0) & (x == ring) & (c == x // 2)
    self_e = (y == 3) & (x // 2 == c)
    greet(at(x, y, z, 1 - c))
    greet(at(x, y, pair_z, c))
    for k in range(1, NX):
        greet(at(turn(k), y, z, c))
    for r in range(NX):
        for e in range(2):
            @pl.when(jnp.logical_not((x == r) & (2 * x + e == z)))
            def _():
                greet(at(r, y, 2 * x + e, c))

    @pl.when(y > 0)
    def _():
        greet(at(x, 0, z, c))
        for r in range(NX):
            for e in range(2):
                greet(at(r, y - 1, 2 * x + e, c))

    @pl.when(y == 0)
    def _():
        for f in range(M):
            for gg in range(2):
                for e in range(2):
                    for cc in range(2):
                        if f == 0:
                            @pl.when(jnp.logical_not((2 * c + gg == x) & (2 * x + e == z) & (c == cc)))
                            def _():
                                greet(at(2 * c + gg, f, 2 * x + e, cc))
                        else:
                            greet(at(2 * c + gg, f, 2 * x + e, cc))

    for b in range(2):
        for cc in range(2):
            @pl.when(jnp.logical_not((y == 3) & (2 * c + b == x) & (c == cc)))
            def _():
                greet(at(2 * c + b, 3, z, cc))

    seg[x] = jnp.zeros((8, 128), I32)
    seg[x, 0:4, 0:MB] = segs[0]
    lane = iota((8, 128), 1)
    table = jnp.full((8, 128), -1, I32)
    for t in range(2):
        for i in range(3):
            who = owner[t, i]
            rank = jnp.int32(0)
            for before in range(i):
                rank = rank + (owner[t, before] == who).astype(I32)
            table = jnp.where(lane == 3 * t + i, 2 * who + rank, table)
    code[x] = table

    count = 21 + jnp.where(y == 0, 3, 0) - self_mx.astype(I32) - self_pro.astype(I32)
    count = count + jnp.where(y < 3, 8, 16) - self_e.astype(I32)
    pl.semaphore_wait(barrier, count)

    def start_pairs():
        loads[1].wait()
        loads[2].wait()
        mine = kvt.at[quad]
        remote(mine, mine, kv_s.at[0], kv_r.at[0], at(x, y, pair_z, c)).start()
        remote(mine, mine, kv_s.at[1], kv_r.at[1], at(x, y, z, 1 - c)).start()

    def start_core():
        loads[3].wait()
        remote(wq_v.at[c], wq_v.at[c], one_s.at[0], one_r.at[0], at(x, y, z, 1 - c)).start()
        loads[4].wait()
        remote(wo_v.at[c], wo_v.at[c], one_s.at[1], one_r.at[1], at(x, y, z, 1 - c)).start()

    loads[0].wait()
    for k in (2, 1, 3):
        remote(raw.at[x], raw.at[x], x3_s.at[0], x3_r.at[0], at(turn(k), y, z, c)).start()
    start_pairs()
    for k in range(1, NX):
        remote(seg.at[x], seg.at[x], x3_s.at[1], x3_r.at[1], at(turn(k), y, z, c)).start()
        remote(code.at[x], code.at[x], x3_s.at[2], x3_r.at[2], at(turn(k), y, z, c)).start()
    start_core()

    settle(raw.at[0:3], x3_r.at[0])
    dest = row_dest[...].astype(F32)
    spread = [
        (iota((24, MB), 0) + 24 * t == iota((24, MB), 1)).astype(F32) for t in range(2)
    ]
    dest = dot(dest[:, 0, :], spread[0]) + dot(dest[:, 1, :], spread[1])
    slot = iota((MB, MB), 0)
    place = iota((MB, MB), 1)
    upper = slot >= 24
    wanted = (slot - jnp.where(upper, 24, 0) + 24 * x).astype(F32)
    same_half = upper == (place >= 24)
    order = jnp.zeros((MB, BLK), F32)
    for l in range(NX):
        hits = same_half & (dest[l : l + 1, :] == wanted)
        order = order + dot(hits.astype(BF16), raw[l])
    packed[...] = order.astype(BF16)
    step = 2 * y + x % 2
    first = hid.at[step, quad]

    @pl.when(y > 0)
    def _():
        pl.semaphore_wait(go, 1)

    for dz in FAR:
        remote(
            packed, first, pro_s.at[1], h_r.at[step], at(ring, 0, (z + dz) % NZ, x // 2)
        ).start()

    @pl.when(self_pro)
    def _():
        local(packed, first, h_r.at[step]).start()

    @pl.when(jnp.logical_not(self_pro))
    def _():
        remote(packed, first, pro_s.at[0], h_r.at[step], at(ring, 0, z, x // 2)).start()

    settle(kvt.at[0], kv_r.at[0])
    other = kvt.at[2 - 2 * odd + c]
    remote(other, other, kv_s.at[2], kv_r.at[2], at(x, y, z, 1 - c)).start()
    settle(kvt.at[0], kv_r.at[1])
    settle(kvt.at[0], kv_r.at[2])
    for t in range(2):
        wkv_v[:, 128 * t : 128 * t + 128] = jnp.concatenate(
            [kvt[j, t] for j in range(4)], axis=0
        ).T
    settle(wq_v.at[0], one_r.at[0])
    settle(wo_v.at[0], one_r.at[1])
    settle(seg.at[0:3], x3_r.at[1])
    settle(code.at[0:3], x3_r.at[2])

    def project(t):
        settle(hid.at[t], h_r.at[t])
        squares = jnp.zeros((MB, 128), F32)
        sums = [jnp.zeros((MB, 256), F32) for _ in range(3)]
        for j in range(4):
            h = hid[t, j].astype(F32)
            square = h * h
            for i in range(4):
                squares = squares + square[:, 128 * i : 128 * i + 128]
            g = gain[:, pl.ds(pl.multiple_of(x * 2048 + BLK * j, BLK), BLK)]
            gated = (h * g).astype(BF16)
            ks = slice(BLK * j, BLK * j + BLK)
            sums[0] = sums[0] + dot(gated, wq_v[0, ks])
            sums[1] = sums[1] + dot(gated, wq_v[1, ks])
            sums[2] = sums[2] + dot(gated, wkv_v[ks])
        total = jnp.sum(squares, axis=1, keepdims=True)
        s_out[t] = jnp.broadcast_to(to_row(total), (8, 128))
        for r in range(NX):
            q_out[t, r, :, 0:128] = sums[r // 2][:, 128 * (r % 2) : 128 * (r % 2) + 128].astype(BF16)
            q_out[t, r, :, 128:384] = sums[2].astype(BF16)
        for k in (2, 1, 3):
            to = turn(k)
            remote(
                q_out.at[t, to], q_in.at[t, k - 1], q_s.at[t], q_r.at[t], at(to, y, z, c)
            ).start()
            remote(
                s_out.at[t], s_in.at[t, k - 1], s_s.at[t], s_r.at[t], at(to, y, z, c)
            ).start()

    def attend(t):
        settle(s_in.at[t], s_r.at[t])
        settle(q_in.at[t], q_r.at[t])
        squares = s_out[t] + s_in[t, 0] + s_in[t, 1] + s_in[t, 2]
        scale = lax.rsqrt(to_col(squares[0:1, 0:MB]) / D + EPS)
        qkv = q_out[t, x].astype(F32)
        for k in range(3):
            qkv = qkv + q_in[t, k].astype(F32)
        qkv = (qkv * scale).astype(BF16)
        scores = dot_nt(qkv[:, 0:128], qkv[:, 128:256]) * HD ** (-0.5)
        seg_row = seg[2 * c + t % 2, pl.ds(t // 2, 1), :][:, 0:MB].astype(F32)
        allowed = (to_col(seg_row) == seg_row) & (iota((MB, MB), 1) <= iota((MB, MB), 0))
        scores = jnp.where(allowed, scores, -jnp.inf)
        weights = jnp.exp(scores - jnp.max(scores, axis=1, keepdims=True))
        probs = (weights / jnp.sum(weights, axis=1, keepdims=True)).astype(BF16)
        mx[t] = dot(probs, qkv[:, 256:384]).astype(BF16)
        place = mixed.at[t, 4 * odd + x]
        for dz in FAR:
            remote(
                mx.at[t], place, mx_s.at[1, t], mx_r.at[t], at(ring, y, (z + dz) % NZ, c)
            ).start()

        @pl.when(self_mx)
        def _():
            local(mx.at[t], place, mx_r.at[t]).start()

        @pl.when(jnp.logical_not(self_mx))
        def _():
            remote(mx.at[t], place, mx_s.at[0, t], mx_r.at[t], at(ring, y, z, c)).start()

    def back(t):
        settle(mixed.at[t], mx_r.at[t])
        whole = jnp.concatenate([mixed[t, j] for j in range(8)], axis=1)
        for jj in range(2):
            sums = dot(whole, wo_v[jj])
            kept = hid[t, 2 * odd + jj].astype(F32)
            sums = (sums + jnp.where(x == ring, kept, 0.0)).astype(BF16)
            for i in range(2):
                o_out[t, 2 * jj + i] = sums[:, 256 * i : 256 * i + 256]
        for k in (2, 1, 3):
            to = turn(k)
            remote(
                o_out.at[t, to], o_in.at[t, k - 1], o_s.at[t], o_r.at[t], at(to, y, z, c)
            ).start()

    def forward(t):
        settle(o_in.at[t], o_r.at[t])
        new = o_out[t, x].astype(F32)
        for k in range(3):
            new = new + o_in[t, k].astype(F32)
        new = new.astype(BF16)

        @pl.when(y < 3)
        def _():
            h_out[t] = new
            lanes = pl.ds(pl.multiple_of(256 * (x % 2), 256), 256)
            for dz in FAR + (0,):
                remote(
                    h_out.at[t], hid.at[t, 2 * odd + x // 2, :, lanes], h_s.at[t], h_r.at[t],
                    at(ring, y + 1, (z + dz) % NZ, c),
                ).start()

        @pl.when(y == 3)
        def _():
            group = 2 * c + t % 2
            seg_row = seg[group, pl.ds(t // 2, 1), :][:, 0:MB]
            hits = seg_row == iota((16, MB), 0)
            amount = jnp.maximum(jnp.sum(hits.astype(F32), axis=1, keepdims=True), 1.0)
            e_out[t] = (dot(hits.astype(BF16), new) / amount).astype(BF16)
            place = e_in.at[x % 2, group]
            for k in (2, 1, 3):
                remote(
                    e_out.at[t], place, e_s.at[1, t], e_r, at(turn(k), t // 2, z, x // 2)
                ).start()
            is_self = (t // 2 == 3) & (x // 2 == c)

            @pl.when(is_self)
            def _():
                local(e_out.at[t], place, e_r).start()

            @pl.when(jnp.logical_not(is_self))
            def _():
                remote(e_out.at[t], place, e_s.at[0, t], e_r, at(x, t // 2, z, x // 2)).start()

    def tick(i, carry):
        @pl.when(i < T)
        def _():
            project(i)

        @pl.when((y == 0) & (i < T - 2) & (i % 2 == 0))
        def _():
            pl.semaphore_signal(
                go, inc=1, device_id=at(x, i // 2 + 1, z, c), device_id_type=MESH
            )

        @pl.when(i > 1)
        def _():
            forward(i - 2)

        @pl.when(i < T)
        def _():
            attend(i)

        @pl.when((i > 0) & (i <= T))
        def _():
            back(i - 1)

        return carry

    lax.fori_loop(0, T + 2, tick, 0)

    settle(raw.at[0:3], x3_s.at[0])
    settle(seg.at[0:3], x3_s.at[1])
    settle(code.at[0:3], x3_s.at[2])
    settle(wq_v.at[0], one_s.at[0])
    settle(wo_v.at[0], one_s.at[1])
    for k in range(3):
        settle(kvt.at[0], kv_s.at[k])

    @pl.when(jnp.logical_not(self_pro))
    def _():
        settle(packed, pro_s.at[0])

    settle(hid.at[0], pro_s.at[1])
    settle(hid.at[0, 0:3], pro_s.at[1])

    def drain(t, carry):
        settle(q_in.at[t], q_s.at[t])
        settle(s_in.at[t], s_s.at[t])
        settle(o_in.at[t], o_s.at[t])
        settle(mixed.at[t, 0:7], mx_s.at[1, t])

        @pl.when(jnp.logical_not(self_mx))
        def _():
            settle(mx.at[t], mx_s.at[0, t])

        @pl.when(y < 3)
        def _():
            settle(hid.at[t], h_s.at[t])

        @pl.when(y == 3)
        def _():
            settle(e_in.at[0, 0:3], e_s.at[1, t])

            @pl.when(jnp.logical_not((t // 2 == 3) & (x // 2 == c)))
            def _():
                settle(e_in.at[0, 0], e_s.at[0, t])

        return carry

    lax.fori_loop(0, T, drain, 0)

    settle(e_in, e_r)
    row = iota((16, 16), 0)
    col = iota((16, 16), 1)
    picked = [jnp.zeros((16, 256), F32) for _ in range(2)]
    for g in range(NX):
        hits = ((row >> 1) & 3) == g
        hits = hits & ((row >= 8) == (col >= 3)) & (col < 6)
        hits = (hits & (code[g, 0:1, 0:16] == 2 * x + (row & 1))).astype(BF16)
        for i in range(2):
            picked[i] = picked[i] + dot(hits, e_in[i, g])
    for i in range(2):
        out[:, 256 * i : 256 * i + 256] = picked[i].astype(BF16)


def shards(prompt_rows, row_dest, segment_ids, owner, gain, w_query, w_key, w_value, w_out):
    any_spec = pl.BlockSpec(memory_space=pl.ANY)
    vmem = pl.BlockSpec(memory_space=pltpu.VMEM)
    smem = pl.BlockSpec(memory_space=pltpu.SMEM)
    dma = pltpu.SemaphoreType.DMA
    embedded = pl.pallas_call(
        kernel,
        out_shape=jax.ShapeDtypeStruct((16, BLK), BF16),
        in_specs=[any_spec, vmem, vmem, smem, vmem, any_spec, any_spec, any_spec, any_spec],
        out_specs=vmem,
        scratch_shapes=[
            pltpu.VMEM((NX, MB, BLK), BF16),
            pltpu.VMEM((NX, 8, 128), I32),
            pltpu.VMEM((NX, 8, 128), I32),
            pltpu.VMEM((2, 2048, 256), BF16),
            pltpu.VMEM((4, 2, 32, 2048), BF16),
            pltpu.VMEM((2048, 256), BF16),
            pltpu.VMEM((2, 1024, BLK), BF16),
            pltpu.VMEM((MB, BLK), BF16),
            pltpu.VMEM((T, 4, MB, BLK), BF16),
            pltpu.VMEM((T, 4, MB, 384), BF16),
            pltpu.VMEM((T, 3, MB, 384), BF16),
            pltpu.VMEM((T, 8, 128), F32),
            pltpu.VMEM((T, 3, 8, 128), F32),
            pltpu.VMEM((T, MB, 128), BF16),
            pltpu.VMEM((T, 8, MB, 128), BF16),
            pltpu.VMEM((T, 4, MB, 256), BF16),
            pltpu.VMEM((T, 3, MB, 256), BF16),
            pltpu.VMEM((T, MB, 256), BF16),
            pltpu.VMEM((T, 16, 256), BF16),
            pltpu.VMEM((2, NX, 16, 256), BF16),
            dma((5,)),
            dma((2,)),
            dma((2,)),
            dma((3,)),
            dma((3,)),
            dma((3,)),
            dma((3,)),
            dma((2,)),
            dma((T,)),
            dma((T,)),
            dma((T,)),
            dma((T,)),
            dma((T,)),
            dma((2, T)),
            dma((T,)),
            dma((T,)),
            dma((T,)),
            dma((T,)),
            dma((2, T)),
            dma,
            pltpu.SemaphoreType.REGULAR,
        ],
        compiler_params=pltpu.CompilerParams(
            collective_id=0, has_side_effects=True, vmem_limit_bytes=60 << 20
        ),
        name="sections",
    )(
        prompt_rows.reshape(MB, BLK),
        row_dest,
        segment_ids,
        owner.reshape(2, 3),
        gain,
        w_query[0],
        w_key[0].T,
        w_value[0].T,
        w_out[0],
    )
    return embedded.reshape(1, 2, 8, BLK)


def solution(mesh):
    in_specs = (
        P("dp", "phase", None, "mp"),
        P(None, "phase", None),
        P("dp", None, None),
        P("dp", "phase", None, None),
        P("phase", None),
        P("phase", "dp", "mp"),
        P("phase", "dp", "mp"),
        P("phase", "dp", "mp"),
        P("phase", "dp", "mp"),
    )
    out_specs = P("dp", "phase", None, "mp")
    return jax.shard_map(shards, mesh=mesh, in_specs=in_specs, out_specs=out_specs, check_vma=False)
```

```python
import jax
import jax.numpy as jnp
from jax import lax
from jax.experimental import pallas as pl
from jax.experimental.pallas import tpu as pltpu
from jax.sharding import PartitionSpec as P

MESH = pl.DeviceIdType.MESH
F32 = jnp.float32
BF16 = jnp.bfloat16
I32 = jnp.int32

D = 8192
HD = 128
MB = 48
M = 4
NX = 4
NZ = 8
EPS = 1e-05
BLK = 512
T = 2 * M
FAR = (4, 3, 5, 2, 6, 1, 7)

ORDERS = (
    "PPAPABPABFPABFPABFPABFPABFABFBFF",
    "PAPABPFABPFABPFABPFBPAFPABABFBFF",
    "PAPABPFABPFABPFABPFBPAFPABABFBFF",
    "PAPABPFABPFABPFABPFBPAFPABABFBFF",
)


def iota(shape, dim):
    return lax.broadcasted_iota(I32, shape, dim)


def dot(a, b):
    return jnp.dot(a, b, preferred_element_type=F32)


def dot_nt(a, b):
    return lax.dot_general(a, b, (((1,), (1,)), ((), ())), preferred_element_type=F32)


def to_row(col):
    eye = iota((MB, 128), 0) == iota((MB, 128), 1)
    return jnp.sum(jnp.where(eye, col, 0.0), axis=0, keepdims=True)


def to_col(row):
    eye = iota((MB, MB), 0) == iota((MB, MB), 1)
    return jnp.sum(jnp.where(eye, row, 0.0), axis=1, keepdims=True)


def kernel(
    rows, row_dest, segs, owner, gain, wq, wk, wv, wo, out,
    raw, seg, code, wq_v, kvt, wkv_v, wo_v, packed, staged,
    hid, q_out, q_in, s_out, s_in, mx, mixed, o_out, o_in, h_out, e_out, e_in,
    loc, one_s, one_r, x3_s, x3_r, kv_s, kv_r, pro_s, h_r,
    q_s, q_r, s_s, s_r, mx_s, mx_r, o_s, o_r, h_s, e_s, e_r, go, st_s, st_r,
):
    x = lax.axis_index("dp")
    y = lax.axis_index("phase")
    p = lax.axis_index("mp")
    z = p // 2
    c = p % 2
    ring = z // 2
    odd = z % 2

    def at(xx, yy, zz, cc):
        return (xx, yy, zz * 2 + cc)

    def remote(src, dst, send, recv, device):
        return pltpu.make_async_remote_copy(
            src_ref=src, dst_ref=dst, send_sem=send, recv_sem=recv,
            device_id=device, device_id_type=MESH,
        )

    def local(src, dst, sem):
        return pltpu.make_async_copy(src, dst, sem)

    def settle(ref, sem):
        pltpu.make_async_copy(ref, ref, sem).wait()

    def turn(k):
        return (x + k) % NX

    quad = 2 * odd + c

    def half_of(k):
        return pl.ds(pl.multiple_of(256 * (k % 2), 256), 256)

    loads = [
        local(rows.at[:, half_of(x)], raw.at[x], loc.at[0]),
        local(wk, kvt.at[quad, 0], loc.at[1]),
        local(wv, kvt.at[quad, 1], loc.at[2]),
        local(wq, wq_v.at[c], loc.at[3]),
        local(wo, wo_v.at[c], loc.at[4]),
    ]
    for load in loads:
        load.start()

    barrier = pltpu.get_barrier_semaphore()

    def greet(device):
        pl.semaphore_signal(barrier, inc=1, device_id=device, device_id_type=MESH)

    pair_z = z + 1 - 2 * odd
    self_mx = x == ring
    self_pro = (y == 0) & (x == ring) & (c == x // 2)
    self_e = (y == 3) & (x // 2 == c)
    from_x, from_z, from_c = 2 * c + z % 2, 2 * x + z // 4, (z // 2) % 2
    self_st = (from_x == x) & (from_z == z) & (from_c == c)
    to_z = 4 * odd + 2 * c + x % 2
    greet(at(x, y, z, 1 - c))
    greet(at(x, y, pair_z, c))
    for k in range(1, NX):
        greet(at(turn(k), y, z, c))
    for r in range(NX):
        for e in range(2):
            @pl.when(jnp.logical_not((x == r) & (2 * x + e == z)))
            def _():
                greet(at(r, y, 2 * x + e, c))

    @pl.when(y > 0)
    def _():
        greet(at(x, 0, z, c))
        for r in range(NX):
            for e in range(2):
                greet(at(r, y - 1, 2 * x + e, c))

    @pl.when(y == 0)
    def _():
        for gg in range(2):
            for e in range(2):
                for cc in range(2):
                    @pl.when(jnp.logical_not((2 * c + gg == x) & (2 * x + e == z) & (c == cc)))
                    def _():
                        greet(at(2 * c + gg, 0, 2 * x + e, cc))
        for f in range(1, M):
            for zz in range(NZ):
                greet(at(x, f, zz, c))

    @pl.when((y > 0) & jnp.logical_not(self_st))
    def _():
        greet(at(from_x, y, from_z, from_c))

    for b in range(2):
        for cc in range(2):
            @pl.when(jnp.logical_not((y == 3) & (2 * c + b == x) & (c == cc)))
            def _():
                greet(at(2 * c + b, 3, z, cc))

    seg[x] = jnp.zeros((8, 128), I32)
    seg[x, 0:4, 0:MB] = segs[0]
    lane = iota((8, 128), 1)
    table = jnp.full((8, 128), -1, I32)
    for t in range(2):
        for i in range(3):
            who = owner[t, i]
            rank = jnp.int32(0)
            for before in range(i):
                rank = rank + (owner[t, before] == who).astype(I32)
            table = jnp.where(lane == 3 * t + i, 2 * who + rank, table)
    code[x] = table

    count = 21 + jnp.where(y == 0, 3, jnp.where(self_st, 0, 1)) - self_mx.astype(I32) - self_pro.astype(I32)
    count = count + jnp.where(y < 3, 8, 16) - self_e.astype(I32)
    pl.semaphore_wait(barrier, count)

    def start_pairs():
        loads[1].wait()
        loads[2].wait()
        mine = kvt.at[quad]
        remote(mine, mine, kv_s.at[0], kv_r.at[0], at(x, y, pair_z, c)).start()
        remote(mine, mine, kv_s.at[1], kv_r.at[1], at(x, y, z, 1 - c)).start()

    def start_core():
        loads[3].wait()
        remote(wq_v.at[c], wq_v.at[c], one_s.at[0], one_r.at[0], at(x, y, z, 1 - c)).start()
        loads[4].wait()
        remote(wo_v.at[c], wo_v.at[c], one_s.at[1], one_r.at[1], at(x, y, z, 1 - c)).start()

    for k in (2, 1, 3):
        to = turn(k)
        remote(
            rows.at[:, half_of(to)], raw.at[x], x3_s.at[0], x3_r.at[0], at(to, y, z, c)
        ).start()
    start_pairs()
    for k in range(1, NX):
        remote(seg.at[x], seg.at[x], x3_s.at[1], x3_r.at[1], at(turn(k), y, z, c)).start()
        remote(code.at[x], code.at[x], x3_s.at[2], x3_r.at[2], at(turn(k), y, z, c)).start()
    start_core()

    dest = row_dest[...].astype(F32)
    spread = [
        (iota((24, MB), 0) + 24 * t == iota((24, MB), 1)).astype(F32) for t in range(2)
    ]
    dest = dot(dest[:, 0, :], spread[0]) + dot(dest[:, 1, :], spread[1])
    slot = iota((MB, MB), 0)
    place = iota((MB, MB), 1)
    upper = slot >= 24
    slot = slot - jnp.where(upper, 24, 0)
    same_half = upper == (place >= 24)
    loads[0].wait()
    settle(raw.at[0:3], x3_r.at[0])

    for h in range(2):
        wanted = (slot + 24 * (h + 2 * (x // 2))).astype(F32)
        order = jnp.zeros((MB, 256), F32)
        for l in range(NX):
            hits = same_half & (dest[l : l + 1, :] == wanted)
            order = order + dot(hits.astype(BF16), raw[l])
        packed[h] = order.astype(BF16)

        @pl.when(y == 0)
        def _():
            first = hid.at[h, quad, :, half_of(x)]
            for dz in FAR:
                remote(
                    packed.at[h], first, pro_s.at[1, h], h_r.at[h],
                    at(ring, 0, (z + dz) % NZ, x // 2),
                ).start()

            @pl.when(self_pro)
            def _():
                local(packed.at[h], first, h_r.at[h]).start()

            @pl.when(jnp.logical_not(self_pro))
            def _():
                remote(
                    packed.at[h], first, pro_s.at[0, h], h_r.at[h], at(ring, 0, z, x // 2)
                ).start()

        @pl.when((y > 0) & self_st)
        def _():
            local(packed.at[h], staged.at[h], st_r).start()

        @pl.when((y > 0) & jnp.logical_not(self_st))
        def _():
            remote(
                packed.at[h], staged.at[h], st_s.at[h], st_r, at(ring, y, to_z, x // 2)
            ).start()

    settle(kvt.at[0], kv_r.at[0])
    other = kvt.at[2 - 2 * odd + c]
    remote(other, other, kv_s.at[2], kv_r.at[2], at(x, y, z, 1 - c)).start()
    settle(kvt.at[0], kv_r.at[1])
    settle(kvt.at[0], kv_r.at[2])
    for t in range(2):
        wkv_v[:, 128 * t : 128 * t + 128] = jnp.concatenate(
            [kvt[j, t] for j in range(4)], axis=0
        ).T
    settle(wq_v.at[0], one_r.at[0])
    settle(wo_v.at[0], one_r.at[1])

    @pl.when(y > 0)
    def _():
        settle(staged, st_r)
        pl.semaphore_wait(go, 1)
        for h in range(2):
            first = hid.at[2 * y + h, 2 * (z // 4) + (z // 2) % 2, :, half_of(z)]
            for dz in FAR + (0,):
                remote(
                    staged.at[h], first, pro_s.at[1, h], h_r.at[2 * y + h],
                    at(x, 0, (z + dz) % NZ, c),
                ).start()

    settle(seg.at[0:3], x3_r.at[1])
    settle(code.at[0:3], x3_r.at[2])

    def project(t):
        settle(hid.at[t], h_r.at[t])
        squares = jnp.zeros((MB, 128), F32)
        sums = [jnp.zeros((MB, 256), F32) for _ in range(3)]
        for j in range(4):
            h = hid[t, j].astype(F32)
            square = h * h
            for i in range(4):
                squares = squares + square[:, 128 * i : 128 * i + 128]
            g = gain[:, pl.ds(pl.multiple_of(x * 2048 + BLK * j, BLK), BLK)]
            gated = (h * g).astype(BF16)
            ks = slice(BLK * j, BLK * j + BLK)
            sums[0] = sums[0] + dot(gated, wq_v[0, ks])
            sums[1] = sums[1] + dot(gated, wq_v[1, ks])
            sums[2] = sums[2] + dot(gated, wkv_v[ks])
        total = jnp.sum(squares, axis=1, keepdims=True)
        s_out[t] = jnp.broadcast_to(to_row(total), (8, 128))
        for r in range(NX):
            q_out[t, r, :, 0:128] = sums[r // 2][:, 128 * (r % 2) : 128 * (r % 2) + 128].astype(BF16)
            q_out[t, r, :, 128:384] = sums[2].astype(BF16)
        for k in (2, 1, 3):
            to = turn(k)
            remote(
                q_out.at[t, to], q_in.at[t, k - 1], q_s.at[t], q_r.at[t], at(to, y, z, c)
            ).start()
            remote(
                s_out.at[t], s_in.at[t, k - 1], s_s.at[t], s_r.at[t], at(to, y, z, c)
            ).start()

    def attend(t):
        settle(s_in.at[t], s_r.at[t])
        settle(q_in.at[t], q_r.at[t])
        squares = s_out[t] + s_in[t, 0] + s_in[t, 1] + s_in[t, 2]
        scale = lax.rsqrt(to_col(squares[0:1, 0:MB]) / D + EPS)
        qkv = q_out[t, x].astype(F32)
        for k in range(3):
            qkv = qkv + q_in[t, k].astype(F32)
        qkv = (qkv * scale).astype(BF16)
        scores = dot_nt(qkv[:, 0:128], qkv[:, 128:256]) * HD ** (-0.5)
        seg_row = seg[2 * c + t % 2, pl.ds(t // 2, 1), :][:, 0:MB].astype(F32)
        allowed = (to_col(seg_row) == seg_row) & (iota((MB, MB), 1) <= iota((MB, MB), 0))
        scores = jnp.where(allowed, scores, -jnp.inf)
        weights = jnp.exp(scores - jnp.max(scores, axis=1, keepdims=True))
        probs = (weights / jnp.sum(weights, axis=1, keepdims=True)).astype(BF16)
        mx[t] = dot(probs, qkv[:, 256:384]).astype(BF16)
        place = mixed.at[t, 4 * odd + x]
        for dz in FAR:
            remote(
                mx.at[t], place, mx_s.at[1, t], mx_r.at[t], at(ring, y, (z + dz) % NZ, c)
            ).start()

        @pl.when(self_mx)
        def _():
            local(mx.at[t], place, mx_r.at[t]).start()

        @pl.when(jnp.logical_not(self_mx))
        def _():
            remote(mx.at[t], place, mx_s.at[0, t], mx_r.at[t], at(ring, y, z, c)).start()

    def back(t):
        settle(mixed.at[t], mx_r.at[t])
        whole = jnp.concatenate([mixed[t, j] for j in range(8)], axis=1)
        for jj in range(2):
            sums = dot(whole, wo_v[jj])
            kept = hid[t, 2 * odd + jj].astype(F32)
            sums = (sums + jnp.where(x == ring, kept, 0.0)).astype(BF16)
            for i in range(2):
                o_out[t, 2 * jj + i] = sums[:, 256 * i : 256 * i + 256]
        for k in (2, 1, 3):
            to = turn(k)
            remote(
                o_out.at[t, to], o_in.at[t, k - 1], o_s.at[t], o_r.at[t], at(to, y, z, c)
            ).start()

    def forward(t):
        settle(o_in.at[t], o_r.at[t])
        new = o_out[t, x].astype(F32)
        for k in range(3):
            new = new + o_in[t, k].astype(F32)
        new = new.astype(BF16)

        @pl.when(y < 3)
        def _():
            h_out[t] = new
            for dz in FAR + (0,):
                remote(
                    h_out.at[t], hid.at[t, 2 * odd + x // 2, :, half_of(x)], h_s.at[t], h_r.at[t],
                    at(ring, y + 1, (z + dz) % NZ, c),
                ).start()

        @pl.when(y == 3)
        def _():
            group = 2 * c + t % 2
            seg_row = seg[group, pl.ds(t // 2, 1), :][:, 0:MB]
            hits = seg_row == iota((16, MB), 0)
            amount = jnp.maximum(jnp.sum(hits.astype(F32), axis=1, keepdims=True), 1.0)
            e_out[t] = (dot(hits.astype(BF16), new) / amount).astype(BF16)
            place = e_in.at[x % 2, group]
            for k in (2, 1, 3):
                remote(
                    e_out.at[t], place, e_s.at[1, t], e_r, at(turn(k), t // 2, z, x // 2)
                ).start()
            is_self = (t // 2 == 3) & (x // 2 == c)

            @pl.when(is_self)
            def _():
                local(e_out.at[t], place, e_r).start()

            @pl.when(jnp.logical_not(is_self))
            def _():
                remote(e_out.at[t], place, e_s.at[0, t], e_r, at(x, t // 2, z, x // 2)).start()

    def ask(t):
        project(t)

        @pl.when((y == 0) & ((t == 0) | (t == 1) | (t == 3)))
        def _():
            pl.semaphore_signal(
                go, inc=1, device_id=at(x, (t + 3) // 2, z, c), device_id_type=MESH
            )

    stages = (ask, attend, back, forward)

    def word_of(k):
        word = jnp.int32(0)
        for plane, order in enumerate(ORDERS):
            for i in range(4 * T // 8):
                value = sum("PABF".index(s) * 4**n for n, s in enumerate(order[8 * i : 8 * i + 8]))
                word = jnp.where((y == plane) & (k // 8 == i), value, word)
        return word

    def tick(k, state):
        word, *counts = state
        word = jnp.where(k % 8 == 0, word_of(k), word)
        code = word % 4
        for s, stage in enumerate(stages):
            @pl.when(code == s)
            def _():
                stage(counts[s])
        counts = [n + jnp.where(code == s, 1, 0) for s, n in enumerate(counts)]
        return (word // 4, *counts)

    lax.fori_loop(0, 4 * T, tick, (jnp.int32(0),) * 5)

    settle(raw.at[0:3], x3_s.at[0])
    settle(seg.at[0:3], x3_s.at[1])
    settle(code.at[0:3], x3_s.at[2])
    settle(wq_v.at[0], one_s.at[0])
    settle(wo_v.at[0], one_s.at[1])
    for k in range(3):
        settle(kvt.at[0], kv_s.at[k])

    for h in range(2):
        @pl.when(y == 0)
        def _():
            settle(h_out.at[0:7], pro_s.at[1, h])

            @pl.when(jnp.logical_not(self_pro))
            def _():
                settle(packed.at[h], pro_s.at[0, h])

        @pl.when(y > 0)
        def _():
            settle(h_out, pro_s.at[1, h])

            @pl.when(jnp.logical_not(self_st))
            def _():
                settle(packed.at[h], st_s.at[h])

    def drain(t, carry):
        settle(q_in.at[t], q_s.at[t])
        settle(s_in.at[t], s_s.at[t])
        settle(o_in.at[t], o_s.at[t])
        settle(mixed.at[t, 0:7], mx_s.at[1, t])

        @pl.when(jnp.logical_not(self_mx))
        def _():
            settle(mx.at[t], mx_s.at[0, t])

        @pl.when(y < 3)
        def _():
            settle(hid.at[t], h_s.at[t])

        @pl.when(y == 3)
        def _():
            settle(e_in.at[0, 0:3], e_s.at[1, t])

            @pl.when(jnp.logical_not((t // 2 == 3) & (x // 2 == c)))
            def _():
                settle(e_in.at[0, 0], e_s.at[0, t])

        return carry

    lax.fori_loop(0, T, drain, 0)

    settle(e_in, e_r)
    row = iota((16, 16), 0)
    col = iota((16, 16), 1)
    picked = [jnp.zeros((16, 256), F32) for _ in range(2)]
    for g in range(NX):
        hits = ((row >> 1) & 3) == g
        hits = hits & ((row >= 8) == (col >= 3)) & (col < 6)
        hits = (hits & (code[g, 0:1, 0:16] == 2 * x + (row & 1))).astype(BF16)
        for i in range(2):
            picked[i] = picked[i] + dot(hits, e_in[i, g])
    for i in range(2):
        out[:, 256 * i : 256 * i + 256] = picked[i].astype(BF16)


def shards(prompt_rows, row_dest, segment_ids, owner, gain, w_query, w_key, w_value, w_out):
    any_spec = pl.BlockSpec(memory_space=pl.ANY)
    vmem = pl.BlockSpec(memory_space=pltpu.VMEM)
    smem = pl.BlockSpec(memory_space=pltpu.SMEM)
    dma = pltpu.SemaphoreType.DMA
    embedded = pl.pallas_call(
        kernel,
        out_shape=jax.ShapeDtypeStruct((16, BLK), BF16),
        in_specs=[any_spec, vmem, vmem, smem, vmem, any_spec, any_spec, any_spec, any_spec],
        out_specs=vmem,
        scratch_shapes=[
            pltpu.VMEM((NX, MB, 256), BF16),
            pltpu.VMEM((NX, 8, 128), I32),
            pltpu.VMEM((NX, 8, 128), I32),
            pltpu.VMEM((2, 2048, 256), BF16),
            pltpu.VMEM((4, 2, 32, 2048), BF16),
            pltpu.VMEM((2048, 256), BF16),
            pltpu.VMEM((2, 1024, BLK), BF16),
            pltpu.VMEM((2, MB, 256), BF16),
            pltpu.VMEM((2, MB, 256), BF16),
            pltpu.VMEM((T, 4, MB, BLK), BF16),
            pltpu.VMEM((T, 4, MB, 384), BF16),
            pltpu.VMEM((T, 3, MB, 384), BF16),
            pltpu.VMEM((T, 8, 128), F32),
            pltpu.VMEM((T, 3, 8, 128), F32),
            pltpu.VMEM((T, MB, 128), BF16),
            pltpu.VMEM((T, 8, MB, 128), BF16),
            pltpu.VMEM((T, 4, MB, 256), BF16),
            pltpu.VMEM((T, 3, MB, 256), BF16),
            pltpu.VMEM((T, MB, 256), BF16),
            pltpu.VMEM((T, 16, 256), BF16),
            pltpu.VMEM((2, NX, 16, 256), BF16),
            dma((5,)),
            dma((2,)),
            dma((2,)),
            dma((3,)),
            dma((3,)),
            dma((3,)),
            dma((3,)),
            dma((2, 2)),
            dma((T,)),
            dma((T,)),
            dma((T,)),
            dma((T,)),
            dma((T,)),
            dma((2, T)),
            dma((T,)),
            dma((T,)),
            dma((T,)),
            dma((T,)),
            dma((2, T)),
            dma,
            pltpu.SemaphoreType.REGULAR,
            dma((2,)),
            dma,
        ],
        compiler_params=pltpu.CompilerParams(
            collective_id=0, has_side_effects=True, vmem_limit_bytes=60 << 20
        ),
        name="sections",
    )(
        prompt_rows.reshape(MB, BLK),
        row_dest,
        segment_ids,
        owner.reshape(2, 3),
        gain,
        w_query[0],
        w_key[0].T,
        w_value[0].T,
        w_out[0],
    )
    return embedded.reshape(1, 2, 8, BLK)


def solution(mesh):
    in_specs = (
        P("dp", "phase", None, "mp"),
        P(None, "phase", None),
        P("dp", None, None),
        P("dp", "phase", None, None),
        P("phase", None),
        P("phase", "dp", "mp"),
        P("phase", "dp", "mp"),
        P("phase", "dp", "mp"),
        P("phase", "dp", "mp"),
    )
    out_specs = P("dp", "phase", None, "mp")
    return jax.shard_map(shards, mesh=mesh, in_specs=in_specs, out_specs=out_specs, check_vma=False)
```

```python
import jax
import jax.numpy as jnp
from jax import lax
from jax.experimental import pallas as pl
from jax.experimental.pallas import tpu as pltpu
from jax.sharding import PartitionSpec as P

MESH = pl.DeviceIdType.MESH
F32 = jnp.float32
BF16 = jnp.bfloat16
I32 = jnp.int32

D = 8192
HD = 128
MB = 48
M = 4
NX = 4
NZ = 8
EPS = 1e-05
BLK = 512
T = 2 * M
FAR = (4, 3, 5, 2, 6, 1, 7)

ORDERS = (
    "PPAPABPABFPABFPABFPABFPABFABFBFF",
    "PAPABPFABPFABPFABPFBPAFPABABFBFF",
    "PAPABPFABPFABPFABPFBPAFPABABFBFF",
    "PAPABPFABPFABPFABPFBPAFPABABFBFF",
)


def iota(shape, dim):
    return lax.broadcasted_iota(I32, shape, dim)


def dot(a, b):
    return jnp.dot(a, b, preferred_element_type=F32)


def dot_nt(a, b):
    return lax.dot_general(a, b, (((1,), (1,)), ((), ())), preferred_element_type=F32)


def to_row(col):
    eye = iota((MB, 128), 0) == iota((MB, 128), 1)
    return jnp.sum(jnp.where(eye, col, 0.0), axis=0, keepdims=True)


def to_col(row):
    eye = iota((MB, MB), 0) == iota((MB, MB), 1)
    return jnp.sum(jnp.where(eye, row, 0.0), axis=1, keepdims=True)


def kernel(
    rows, row_dest, segs, owner, gain, wq, wk, wv, wo, out,
    raw, seg, code, wq_v, kvt, wkv_v, wo_v, packed, staged,
    hid, q_out, q_in, s_out, s_in, mx, mixed, o_out, o_in, h_out, e_out, e_in,
    loc, one_s, one_r, x3_s, x3_r, kv_s, kv_r, pro_s, h_r,
    q_s, q_r, s_s, s_r, mx_s, mx_r, o_s, o_r, h_s, e_s, e_r, go, st_s, st_r,
):
    x = lax.axis_index("dp")
    y = lax.axis_index("phase")
    p = lax.axis_index("mp")
    z = p // 2
    c = p % 2
    ring = z // 2
    odd = z % 2

    def at(xx, yy, zz, cc):
        return (xx, yy, zz * 2 + cc)

    def remote(src, dst, send, recv, device):
        return pltpu.make_async_remote_copy(
            src_ref=src, dst_ref=dst, send_sem=send, recv_sem=recv,
            device_id=device, device_id_type=MESH,
        )

    def local(src, dst, sem):
        return pltpu.make_async_copy(src, dst, sem)

    def settle(ref, sem):
        pltpu.make_async_copy(ref, ref, sem).wait()

    def turn(k):
        return (x + k) % NX

    quad = 2 * odd + c

    def half_of(k):
        return pl.ds(pl.multiple_of(256 * (k % 2), 256), 256)

    loads = [
        local(rows.at[:, half_of(x)], raw.at[x], loc.at[0]),
        local(wk, kvt.at[quad, 0], loc.at[1]),
        local(wv, kvt.at[quad, 1], loc.at[2]),
        local(wq, wq_v.at[c], loc.at[3]),
        local(wo, wo_v.at[c], loc.at[4]),
    ]
    for load in loads:
        load.start()

    barrier = pltpu.get_barrier_semaphore()

    def greet(device):
        pl.semaphore_signal(barrier, inc=1, device_id=device, device_id_type=MESH)

    pair_z = z + 1 - 2 * odd
    self_mx = x == ring
    self_pro = (y == 0) & (x == ring) & (c == x // 2)
    from_x, from_z, from_c = 2 * c + z % 2, 2 * x + z // 4, (z // 2) % 2
    self_st = (from_x == x) & (from_z == z) & (from_c == c)
    to_z = 4 * odd + 2 * c + x % 2
    greet(at(x, y, z, 1 - c))
    greet(at(x, y, pair_z, c))
    for k in range(1, NX):
        greet(at(turn(k), y, z, c))
    for r in range(NX):
        for e in range(2):
            @pl.when(jnp.logical_not((x == r) & (2 * x + e == z)))
            def _():
                greet(at(r, y, 2 * x + e, c))

    @pl.when(y > 0)
    def _():
        greet(at(x, 0, z, c))
        for r in range(NX):
            for e in range(2):
                greet(at(r, y - 1, 2 * x + e, c))

    @pl.when(y == 0)
    def _():
        for gg in range(2):
            for e in range(2):
                for cc in range(2):
                    @pl.when(jnp.logical_not((2 * c + gg == x) & (2 * x + e == z) & (c == cc)))
                    def _():
                        greet(at(2 * c + gg, 0, 2 * x + e, cc))
        for f in range(1, M):
            for zz in range(NZ):
                greet(at(x, f, zz, c))

    @pl.when((y > 0) & jnp.logical_not(self_st))
    def _():
        greet(at(from_x, y, from_z, from_c))

    for xx in range(NX):
        for cc in range(2):
            @pl.when(jnp.logical_not((y == 3) & (xx == x) & (c == cc)))
            def _():
                greet(at(xx, 3, z, cc))

    seg[x] = jnp.zeros((8, 128), I32)
    seg[x, 0:4, 0:MB] = segs[0]
    lane = iota((8, 128), 1)
    table = jnp.full((8, 128), -1, I32)
    for t in range(2):
        for i in range(3):
            who = owner[t, i]
            rank = jnp.int32(0)
            for before in range(i):
                rank = rank + (owner[t, before] == who).astype(I32)
            table = jnp.where(lane == 3 * t + i, 2 * who + rank, table)
    code[x] = table

    count = 21 + jnp.where(y == 0, 3, jnp.where(self_st, 0, 1)) - self_mx.astype(I32) - self_pro.astype(I32)
    count = count + jnp.where(y < 3, 8, 31)
    pl.semaphore_wait(barrier, count)

    def start_pairs():
        loads[1].wait()
        loads[2].wait()
        mine = kvt.at[quad]
        remote(mine, mine, kv_s.at[0], kv_r.at[0], at(x, y, pair_z, c)).start()
        remote(mine, mine, kv_s.at[1], kv_r.at[1], at(x, y, z, 1 - c)).start()

    def start_core():
        loads[3].wait()
        remote(wq_v.at[c], wq_v.at[c], one_s.at[0], one_r.at[0], at(x, y, z, 1 - c)).start()
        loads[4].wait()
        remote(wo_v.at[c], wo_v.at[c], one_s.at[1], one_r.at[1], at(x, y, z, 1 - c)).start()

    for k in (2, 1, 3):
        to = turn(k)
        remote(
            rows.at[:, half_of(to)], raw.at[x], x3_s.at[0], x3_r.at[0], at(to, y, z, c)
        ).start()
    start_pairs()
    for k in range(1, NX):
        remote(seg.at[x], seg.at[x], x3_s.at[1], x3_r.at[1], at(turn(k), y, z, c)).start()
        remote(code.at[x], code.at[x], x3_s.at[2], x3_r.at[2], at(turn(k), y, z, c)).start()
    start_core()

    dest = row_dest[...].astype(F32)
    spread = [
        (iota((24, MB), 0) + 24 * t == iota((24, MB), 1)).astype(F32) for t in range(2)
    ]
    dest = dot(dest[:, 0, :], spread[0]) + dot(dest[:, 1, :], spread[1])
    slot = iota((MB, MB), 0)
    place = iota((MB, MB), 1)
    upper = slot >= 24
    slot = slot - jnp.where(upper, 24, 0)
    same_half = upper == (place >= 24)
    loads[0].wait()
    settle(raw.at[0:3], x3_r.at[0])

    for h in range(2):
        wanted = (slot + 24 * (h + 2 * (x // 2))).astype(F32)
        order = jnp.zeros((MB, 256), F32)
        for l in range(NX):
            hits = same_half & (dest[l : l + 1, :] == wanted)
            order = order + dot(hits.astype(BF16), raw[l])
        packed[h] = order.astype(BF16)

        @pl.when(y == 0)
        def _():
            first = hid.at[h, quad, :, half_of(x)]
            for dz in FAR:
                remote(
                    packed.at[h], first, pro_s.at[1, h], h_r.at[h],
                    at(ring, 0, (z + dz) % NZ, x // 2),
                ).start()

            @pl.when(self_pro)
            def _():
                local(packed.at[h], first, h_r.at[h]).start()

            @pl.when(jnp.logical_not(self_pro))
            def _():
                remote(
                    packed.at[h], first, pro_s.at[0, h], h_r.at[h], at(ring, 0, z, x // 2)
                ).start()

        @pl.when((y > 0) & self_st)
        def _():
            local(packed.at[h], staged.at[h], st_r).start()

        @pl.when((y > 0) & jnp.logical_not(self_st))
        def _():
            remote(
                packed.at[h], staged.at[h], st_s.at[h], st_r, at(ring, y, to_z, x // 2)
            ).start()

    settle(kvt.at[0], kv_r.at[0])
    other = kvt.at[2 - 2 * odd + c]
    remote(other, other, kv_s.at[2], kv_r.at[2], at(x, y, z, 1 - c)).start()
    settle(kvt.at[0], kv_r.at[1])
    settle(kvt.at[0], kv_r.at[2])
    for t in range(2):
        wkv_v[:, 128 * t : 128 * t + 128] = jnp.concatenate(
            [kvt[j, t] for j in range(4)], axis=0
        ).T
    settle(wq_v.at[0], one_r.at[0])
    settle(wo_v.at[0], one_r.at[1])

    @pl.when(y > 0)
    def _():
        settle(staged, st_r)
        pl.semaphore_wait(go, 1)
        for h in range(2):
            first = hid.at[2 * y + h, 2 * (z // 4) + (z // 2) % 2, :, half_of(z)]
            for dz in FAR + (0,):
                remote(
                    staged.at[h], first, pro_s.at[1, h], h_r.at[2 * y + h],
                    at(x, 0, (z + dz) % NZ, c),
                ).start()

    settle(seg.at[0:3], x3_r.at[1])
    settle(code.at[0:3], x3_r.at[2])

    def project(t):
        settle(hid.at[t], h_r.at[t])
        squares = jnp.zeros((MB, 128), F32)
        sums = [jnp.zeros((MB, 256), F32) for _ in range(3)]
        for j in range(4):
            h = hid[t, j].astype(F32)
            square = h * h
            for i in range(4):
                squares = squares + square[:, 128 * i : 128 * i + 128]
            g = gain[:, pl.ds(pl.multiple_of(x * 2048 + BLK * j, BLK), BLK)]
            gated = (h * g).astype(BF16)
            ks = slice(BLK * j, BLK * j + BLK)
            sums[0] = sums[0] + dot(gated, wq_v[0, ks])
            sums[1] = sums[1] + dot(gated, wq_v[1, ks])
            sums[2] = sums[2] + dot(gated, wkv_v[ks])
        total = jnp.sum(squares, axis=1, keepdims=True)
        s_out[t] = jnp.broadcast_to(to_row(total), (8, 128))
        for r in range(NX):
            q_out[t, r, :, 0:128] = sums[r // 2][:, 128 * (r % 2) : 128 * (r % 2) + 128].astype(BF16)
            q_out[t, r, :, 128:384] = sums[2].astype(BF16)
        for k in (2, 1, 3):
            to = turn(k)
            remote(
                q_out.at[t, to], q_in.at[t, k - 1], q_s.at[t], q_r.at[t], at(to, y, z, c)
            ).start()
            remote(
                s_out.at[t], s_in.at[t, k - 1], s_s.at[t], s_r.at[t], at(to, y, z, c)
            ).start()

    def attend(t):
        settle(s_in.at[t], s_r.at[t])
        settle(q_in.at[t], q_r.at[t])
        squares = s_out[t] + s_in[t, 0] + s_in[t, 1] + s_in[t, 2]
        scale = lax.rsqrt(to_col(squares[0:1, 0:MB]) / D + EPS)
        qkv = q_out[t, x].astype(F32)
        for k in range(3):
            qkv = qkv + q_in[t, k].astype(F32)
        qkv = (qkv * scale).astype(BF16)
        scores = dot_nt(qkv[:, 0:128], qkv[:, 128:256]) * HD ** (-0.5)
        seg_row = seg[2 * c + t % 2, pl.ds(t // 2, 1), :][:, 0:MB].astype(F32)
        allowed = (to_col(seg_row) == seg_row) & (iota((MB, MB), 1) <= iota((MB, MB), 0))
        scores = jnp.where(allowed, scores, -jnp.inf)
        weights = jnp.exp(scores - jnp.max(scores, axis=1, keepdims=True))
        probs = (weights / jnp.sum(weights, axis=1, keepdims=True)).astype(BF16)
        mx[t] = dot(probs, qkv[:, 256:384]).astype(BF16)
        place = mixed.at[t, 4 * odd + x]
        for dz in FAR:
            remote(
                mx.at[t], place, mx_s.at[1, t], mx_r.at[t], at(ring, y, (z + dz) % NZ, c)
            ).start()

        @pl.when(self_mx)
        def _():
            local(mx.at[t], place, mx_r.at[t]).start()

        @pl.when(jnp.logical_not(self_mx))
        def _():
            remote(mx.at[t], place, mx_s.at[0, t], mx_r.at[t], at(ring, y, z, c)).start()

    def back(t):
        settle(mixed.at[t], mx_r.at[t])
        whole = jnp.concatenate([mixed[t, j] for j in range(8)], axis=1)
        group = 2 * c + t % 2
        seg_row = seg[group, pl.ds(t // 2, 1), :][:, 0:MB]
        hits = seg_row == iota((16, MB), 0)
        amount = jnp.maximum(jnp.sum(hits.astype(F32), axis=1, keepdims=True), 1.0)
        for jj in range(2):
            sums = dot(whole, wo_v[jj])
            kept = hid[t, 2 * odd + jj].astype(F32)
            sums = (sums + jnp.where(x == ring, kept, 0.0)).astype(BF16)

            @pl.when(y < 3)
            def _():
                for i in range(2):
                    o_out[t, 2 * jj + i] = sums[:, 256 * i : 256 * i + 256]

            @pl.when(y == 3)
            def _():
                e_out[t, jj] = (dot(hits.astype(BF16), sums) / amount).astype(BF16)
                place = e_in.at[4 * x + group]
                for k in (2, 1, 3):
                    remote(
                        e_out.at[t, jj], place, e_s.at[1, t], e_r, at(turn(k), t // 2, z, jj)
                    ).start()
                is_self = (t // 2 == 3) & (c == jj)

                @pl.when(is_self)
                def _():
                    local(e_out.at[t, jj], place, e_r).start()

                @pl.when(jnp.logical_not(is_self))
                def _():
                    remote(
                        e_out.at[t, jj], place, e_s.at[0, t], e_r, at(x, t // 2, z, jj)
                    ).start()

        @pl.when(y < 3)
        def _():
            for k in (2, 1, 3):
                to = turn(k)
                remote(
                    o_out.at[t, to], o_in.at[t, k - 1], o_s.at[t], o_r.at[t], at(to, y, z, c)
                ).start()

    def forward(t):
        @pl.when(y < 3)
        def _():
            settle(o_in.at[t], o_r.at[t])
            new = o_out[t, x].astype(F32)
            for k in range(3):
                new = new + o_in[t, k].astype(F32)
            h_out[t] = new.astype(BF16)
            for dz in FAR + (0,):
                remote(
                    h_out.at[t], hid.at[t, 2 * odd + x // 2, :, half_of(x)], h_s.at[t], h_r.at[t],
                    at(ring, y + 1, (z + dz) % NZ, c),
                ).start()

    def ask(t):
        project(t)

        @pl.when((y == 0) & ((t == 0) | (t == 1) | (t == 3)))
        def _():
            pl.semaphore_signal(
                go, inc=1, device_id=at(x, (t + 3) // 2, z, c), device_id_type=MESH
            )

    stages = (ask, attend, back, forward)

    def word_of(k):
        word = jnp.int32(0)
        for plane, order in enumerate(ORDERS):
            for i in range(4 * T // 8):
                value = sum("PABF".index(s) * 4**n for n, s in enumerate(order[8 * i : 8 * i + 8]))
                word = jnp.where((y == plane) & (k // 8 == i), value, word)
        return word

    def tick(k, state):
        word, *counts = state
        word = jnp.where(k % 8 == 0, word_of(k), word)
        code = word % 4
        for s, stage in enumerate(stages):
            @pl.when(code == s)
            def _():
                stage(counts[s])
        counts = [n + jnp.where(code == s, 1, 0) for s, n in enumerate(counts)]
        return (word // 4, *counts)

    lax.fori_loop(0, 4 * T, tick, (jnp.int32(0),) * 5)

    settle(raw.at[0:3], x3_s.at[0])
    settle(seg.at[0:3], x3_s.at[1])
    settle(code.at[0:3], x3_s.at[2])
    settle(wq_v.at[0], one_s.at[0])
    settle(wo_v.at[0], one_s.at[1])
    for k in range(3):
        settle(kvt.at[0], kv_s.at[k])

    for h in range(2):
        @pl.when(y == 0)
        def _():
            settle(h_out.at[0:7], pro_s.at[1, h])

            @pl.when(jnp.logical_not(self_pro))
            def _():
                settle(packed.at[h], pro_s.at[0, h])

        @pl.when(y > 0)
        def _():
            settle(h_out, pro_s.at[1, h])

            @pl.when(jnp.logical_not(self_st))
            def _():
                settle(packed.at[h], st_s.at[h])

    def drain(t, carry):
        settle(q_in.at[t], q_s.at[t])
        settle(s_in.at[t], s_s.at[t])
        settle(mixed.at[t, 0:7], mx_s.at[1, t])

        @pl.when(jnp.logical_not(self_mx))
        def _():
            settle(mx.at[t], mx_s.at[0, t])

        @pl.when(y < 3)
        def _():
            settle(o_in.at[t], o_s.at[t])
            settle(hid.at[t], h_s.at[t])

        @pl.when(y == 3)
        def _():
            settle(e_in.at[0:6], e_s.at[1, t])

            @pl.when(t // 2 < 3)
            def _():
                settle(e_in.at[0:2], e_s.at[0, t])

            @pl.when(t // 2 == 3)
            def _():
                settle(e_in.at[0], e_s.at[0, t])

        return carry

    lax.fori_loop(0, T, drain, 0)

    settle(e_in, e_r)
    row = iota((16, 16), 0)
    col = iota((16, 16), 1)
    picked = jnp.zeros((16, BLK), F32)
    for g in range(NX):
        hits = ((row >> 1) & 3) == g
        hits = hits & ((row >= 8) == (col >= 3)) & (col < 6)
        hits = (hits & (code[g, 0:1, 0:16] == 2 * x + (row & 1))).astype(BF16)
        mean = e_in[g].astype(F32)
        for k in range(1, NX):
            mean = mean + e_in[4 * k + g].astype(F32)
        picked = picked + dot(hits, mean.astype(BF16))
    out[...] = picked.astype(BF16)


def shards(prompt_rows, row_dest, segment_ids, owner, gain, w_query, w_key, w_value, w_out):
    any_spec = pl.BlockSpec(memory_space=pl.ANY)
    vmem = pl.BlockSpec(memory_space=pltpu.VMEM)
    smem = pl.BlockSpec(memory_space=pltpu.SMEM)
    dma = pltpu.SemaphoreType.DMA
    embedded = pl.pallas_call(
        kernel,
        out_shape=jax.ShapeDtypeStruct((16, BLK), BF16),
        in_specs=[any_spec, vmem, vmem, smem, vmem, any_spec, any_spec, any_spec, any_spec],
        out_specs=vmem,
        scratch_shapes=[
            pltpu.VMEM((NX, MB, 256), BF16),
            pltpu.VMEM((NX, 8, 128), I32),
            pltpu.VMEM((NX, 8, 128), I32),
            pltpu.VMEM((2, 2048, 256), BF16),
            pltpu.VMEM((4, 2, 32, 2048), BF16),
            pltpu.VMEM((2048, 256), BF16),
            pltpu.VMEM((2, 1024, BLK), BF16),
            pltpu.VMEM((2, MB, 256), BF16),
            pltpu.VMEM((2, MB, 256), BF16),
            pltpu.VMEM((T, 4, MB, BLK), BF16),
            pltpu.VMEM((T, 4, MB, 384), BF16),
            pltpu.VMEM((T, 3, MB, 384), BF16),
            pltpu.VMEM((T, 8, 128), F32),
            pltpu.VMEM((T, 3, 8, 128), F32),
            pltpu.VMEM((T, MB, 128), BF16),
            pltpu.VMEM((T, 8, MB, 128), BF16),
            pltpu.VMEM((T, 4, MB, 256), BF16),
            pltpu.VMEM((T, 3, MB, 256), BF16),
            pltpu.VMEM((T, MB, 256), BF16),
            pltpu.VMEM((T, 2, 16, BLK), BF16),
            pltpu.VMEM((4 * NX, 16, BLK), BF16),
            dma((5,)),
            dma((2,)),
            dma((2,)),
            dma((3,)),
            dma((3,)),
            dma((3,)),
            dma((3,)),
            dma((2, 2)),
            dma((T,)),
            dma((T,)),
            dma((T,)),
            dma((T,)),
            dma((T,)),
            dma((2, T)),
            dma((T,)),
            dma((T,)),
            dma((T,)),
            dma((T,)),
            dma((2, T)),
            dma,
            pltpu.SemaphoreType.REGULAR,
            dma((2,)),
            dma,
        ],
        compiler_params=pltpu.CompilerParams(
            collective_id=0, has_side_effects=True, vmem_limit_bytes=60 << 20
        ),
        name="sections",
    )(
        prompt_rows.reshape(MB, BLK),
        row_dest,
        segment_ids,
        owner.reshape(2, 3),
        gain,
        w_query[0],
        w_key[0].T,
        w_value[0].T,
        w_out[0],
    )
    return embedded.reshape(1, 2, 8, BLK)


def solution(mesh):
    in_specs = (
        P("dp", "phase", None, "mp"),
        P(None, "phase", None),
        P("dp", None, None),
        P("dp", "phase", None, None),
        P("phase", None),
        P("phase", "dp", "mp"),
        P("phase", "dp", "mp"),
        P("phase", "dp", "mp"),
        P("phase", "dp", "mp"),
    )
    out_specs = P("dp", "phase", None, "mp")
    return jax.shard_map(shards, mesh=mesh, in_specs=in_specs, out_specs=out_specs, check_vma=False)
```

```python
import jax
import jax.numpy as jnp
from jax import lax
from jax.experimental import pallas as pl
from jax.experimental.pallas import tpu as pltpu
from jax.sharding import PartitionSpec as P

MESH = pl.DeviceIdType.MESH
F32 = jnp.float32
BF16 = jnp.bfloat16
I32 = jnp.int32

D = 8192
HD = 128
MB = 48
M = 4
NX = 4
NZ = 8
EPS = 1e-05
BLK = 512
T = 2 * M
FAR = (4, 3, 5, 2, 6, 1, 7)

ORDERS = (
    "PPAPABPABFPABFPABFPABFPABFABFBFF",
    "PAPABPFABPFABPFABPFBPAFPABABFBFF",
    "PAPABPFABPFABPFABPFBPAFPABABFBFF",
    "PAPABPFABPFABPFABPFBPAFPABABFBFF",
)


def iota(shape, dim):
    return lax.broadcasted_iota(I32, shape, dim)


def dot(a, b):
    return jnp.dot(a, b, preferred_element_type=F32)


def dot_nt(a, b):
    return lax.dot_general(a, b, (((1,), (1,)), ((), ())), preferred_element_type=F32)


def to_row(col):
    eye = iota((MB, 128), 0) == iota((MB, 128), 1)
    return jnp.sum(jnp.where(eye, col, 0.0), axis=0, keepdims=True)


def to_col(row):
    eye = iota((MB, MB), 0) == iota((MB, MB), 1)
    return jnp.sum(jnp.where(eye, row, 0.0), axis=1, keepdims=True)


def kernel(
    rows, row_dest, segs, owner, gain, wq, wk, wv, wo, out,
    raw, seg, code, wq_v, kvt, wkv_v, wo_v, packed, staged,
    hid, q_out, q_in, s_out, s_in, mx, mixed, o_out, o_in, h_out, e_out, e_in,
    loc, one_s, one_r, x3_s, x3_r, kv_s, kv_r, pro_s, h_r,
    q_s, q_r, s_s, s_r, mx_s, mx_r, o_s, o_r, h_s, e_s, e_r, go, st_s, st_r,
):
    x = lax.axis_index("dp")
    y = lax.axis_index("phase")
    p = lax.axis_index("mp")
    z = p // 2
    c = p % 2
    ring = z // 2
    odd = z % 2

    def at(xx, yy, zz, cc):
        return (xx, yy, zz * 2 + cc)

    def remote(src, dst, send, recv, device):
        return pltpu.make_async_remote_copy(
            src_ref=src, dst_ref=dst, send_sem=send, recv_sem=recv,
            device_id=device, device_id_type=MESH,
        )

    def local(src, dst, sem):
        return pltpu.make_async_copy(src, dst, sem)

    def settle(ref, sem):
        pltpu.make_async_copy(ref, ref, sem).wait()

    def turn(k):
        return (x + k) % NX

    quad = 2 * odd + c

    def half_of(k):
        return pl.ds(pl.multiple_of(256 * (k % 2), 256), 256)

    loads = [
        local(rows.at[:, half_of(x)], raw.at[x], loc.at[0]),
        local(wk, kvt.at[quad, 0], loc.at[1]),
        local(wv, kvt.at[quad, 1], loc.at[2]),
        local(wq, wq_v.at[c], loc.at[3]),
        local(wo, wo_v.at[c], loc.at[4]),
    ]
    for load in loads:
        load.start()

    barrier = pltpu.get_barrier_semaphore()

    def greet(device):
        pl.semaphore_signal(barrier, inc=1, device_id=device, device_id_type=MESH)

    pair_z = z + 1 - 2 * odd
    self_mx = x == ring
    self_pro = (y == 0) & (x == ring) & (c == x // 2)
    from_x, from_z, from_c = 2 * c + z % 2, 2 * x + z // 4, (z // 2) % 2
    self_st = (from_x == x) & (from_z == z) & (from_c == c)
    to_z = 4 * odd + 2 * c + x % 2
    greet(at(x, y, z, 1 - c))
    greet(at(x, y, pair_z, c))
    for k in range(1, NX):
        greet(at(turn(k), y, z, c))
    for r in range(NX):
        for e in range(2):
            @pl.when(jnp.logical_not((x == r) & (2 * x + e == z)))
            def _():
                greet(at(r, y, 2 * x + e, c))

    @pl.when(y > 0)
    def _():
        greet(at(x, 0, z, c))
        for r in range(NX):
            for e in range(2):
                greet(at(r, y - 1, 2 * x + e, c))

    @pl.when(y == 0)
    def _():
        for gg in range(2):
            for e in range(2):
                for cc in range(2):
                    @pl.when(jnp.logical_not((2 * c + gg == x) & (2 * x + e == z) & (c == cc)))
                    def _():
                        greet(at(2 * c + gg, 0, 2 * x + e, cc))
        for f in range(1, M):
            for zz in range(NZ):
                greet(at(x, f, zz, c))

    @pl.when((y > 0) & jnp.logical_not(self_st))
    def _():
        greet(at(from_x, y, from_z, from_c))

    for xx in range(NX):
        for cc in range(2):
            @pl.when(jnp.logical_not((y == 3) & (xx == x) & (c == cc)))
            def _():
                greet(at(xx, 3, z, cc))

    seg[x] = jnp.zeros((8, 128), I32)
    seg[x, 0:4, 0:MB] = segs[0]
    lane = iota((8, 128), 1)
    table = jnp.full((8, 128), -1, I32)
    for t in range(2):
        for i in range(3):
            who = owner[t, i]
            rank = jnp.int32(0)
            for before in range(i):
                rank = rank + (owner[t, before] == who).astype(I32)
            table = jnp.where(lane == 3 * t + i, 2 * who + rank, table)
    code[x] = table

    count = 21 + jnp.where(y == 0, 3, jnp.where(self_st, 0, 1)) - self_mx.astype(I32) - self_pro.astype(I32)
    count = count + jnp.where(y < 3, 8, 31)
    pl.semaphore_wait(barrier, count)

    def start_pairs():
        loads[1].wait()
        loads[2].wait()
        mine = kvt.at[quad]
        remote(mine, mine, kv_s.at[0], kv_r.at[0], at(x, y, pair_z, c)).start()
        remote(mine, mine, kv_s.at[1], kv_r.at[1], at(x, y, z, 1 - c)).start()

    def start_core():
        loads[3].wait()
        remote(wq_v.at[c], wq_v.at[c], one_s.at[0], one_r.at[0], at(x, y, z, 1 - c)).start()
        loads[4].wait()
        remote(wo_v.at[c], wo_v.at[c], one_s.at[1], one_r.at[1], at(x, y, z, 1 - c)).start()

    for k in (2, 1, 3):
        to = turn(k)
        remote(
            rows.at[:, half_of(to)], raw.at[x], x3_s.at[0], x3_r.at[0], at(to, y, z, c)
        ).start()
    start_pairs()
    for k in range(1, NX):
        remote(seg.at[x], seg.at[x], x3_s.at[1], x3_r.at[1], at(turn(k), y, z, c)).start()
        remote(code.at[x], code.at[x], x3_s.at[2], x3_r.at[2], at(turn(k), y, z, c)).start()
    start_core()

    dest = row_dest[...].astype(F32)
    spread = [
        (iota((24, MB), 0) + 24 * t == iota((24, MB), 1)).astype(F32) for t in range(2)
    ]
    dest = dot(dest[:, 0, :], spread[0]) + dot(dest[:, 1, :], spread[1])
    slot = iota((MB, MB), 0)
    place = iota((MB, MB), 1)
    upper = slot >= 24
    slot = slot - jnp.where(upper, 24, 0)
    same_half = upper == (place >= 24)
    loads[0].wait()
    settle(raw.at[0:3], x3_r.at[0])

    for h in range(2):
        wanted = (slot + 24 * (h + 2 * (x // 2))).astype(F32)
        order = jnp.zeros((MB, 256), F32)
        for l in range(NX):
            hits = same_half & (dest[l : l + 1, :] == wanted)
            order = order + dot(hits.astype(BF16), raw[l])
        packed[h] = order.astype(BF16)

        @pl.when(y == 0)
        def _():
            first = hid.at[h, quad, :, half_of(x)]
            for dz in FAR:
                remote(
                    packed.at[h], first, pro_s.at[1, h], h_r.at[h],
                    at(ring, 0, (z + dz) % NZ, x // 2),
                ).start()

            @pl.when(self_pro)
            def _():
                local(packed.at[h], first, h_r.at[h]).start()

            @pl.when(jnp.logical_not(self_pro))
            def _():
                remote(
                    packed.at[h], first, pro_s.at[0, h], h_r.at[h], at(ring, 0, z, x // 2)
                ).start()

        @pl.when((y > 0) & self_st)
        def _():
            local(packed.at[h], staged.at[h], st_r).start()

        @pl.when((y > 0) & jnp.logical_not(self_st))
        def _():
            remote(
                packed.at[h], staged.at[h], st_s.at[h], st_r, at(ring, y, to_z, x // 2)
            ).start()

    settle(kvt.at[0], kv_r.at[0])
    other = kvt.at[2 - 2 * odd + c]
    remote(other, other, kv_s.at[2], kv_r.at[2], at(x, y, z, 1 - c)).start()
    settle(kvt.at[0], kv_r.at[1])
    settle(kvt.at[0], kv_r.at[2])
    for t in range(2):
        wkv_v[:, 128 * t : 128 * t + 128] = jnp.concatenate(
            [kvt[j, t] for j in range(4)], axis=0
        ).T
    settle(wq_v.at[0], one_r.at[0])
    settle(wo_v.at[0], one_r.at[1])

    @pl.when(y > 0)
    def _():
        settle(staged, st_r)
        pl.semaphore_wait(go, 1)
        for h in range(2):
            first = hid.at[2 * y + h, 2 * (z // 4) + (z // 2) % 2, :, half_of(z)]
            for dz in FAR + (0,):
                remote(
                    staged.at[h], first, pro_s.at[1, h], h_r.at[2 * y + h],
                    at(x, 0, (z + dz) % NZ, c),
                ).start()

    settle(seg.at[0:3], x3_r.at[1])
    settle(code.at[0:3], x3_r.at[2])

    def project(t):
        settle(hid.at[t], h_r.at[t])
        squares = jnp.zeros((MB, 128), F32)
        gated = []
        for j in range(4):
            h = hid[t, j].astype(F32)
            square = h * h
            for i in range(4):
                squares = squares + square[:, 128 * i : 128 * i + 128]
            g = gain[:, pl.ds(pl.multiple_of(x * 2048 + BLK * j, BLK), BLK)]
            gated.append((h * g).astype(BF16))
        total = jnp.sum(squares, axis=1, keepdims=True)
        s_out[t] = jnp.broadcast_to(to_row(total), (8, 128))
        for k in (2, 1, 3):
            remote(
                s_out.at[t], s_in.at[t, k - 1], s_s.at[t], s_r.at[t], at(turn(k), y, z, c)
            ).start()

        def times(weights):
            sums = jnp.zeros((MB, 256), F32)
            for j in range(4):
                sums = sums + dot(gated[j], weights[BLK * j : BLK * j + BLK])
            return sums.astype(BF16)

        pair = times(wkv_v)
        for jj in range(2):
            heads = times(wq_v.at[jj])
            for i in range(2):
                q_out[t, 2 * jj + i, :, 0:128] = heads[:, 128 * i : 128 * i + 128]
                q_out[t, 2 * jj + i, :, 128:384] = pair
            for k in (2, 1, 3):
                to = turn(k)

                @pl.when(to // 2 == jj)
                def _():
                    remote(
                        q_out.at[t, to], q_in.at[t, k - 1], q_s.at[t], q_r.at[t], at(to, y, z, c)
                    ).start()

    def attend(t):
        settle(s_in.at[t], s_r.at[t])
        settle(q_in.at[t], q_r.at[t])
        squares = s_out[t] + s_in[t, 0] + s_in[t, 1] + s_in[t, 2]
        scale = lax.rsqrt(to_col(squares[0:1, 0:MB]) / D + EPS)
        qkv = q_out[t, x].astype(F32)
        for k in range(3):
            qkv = qkv + q_in[t, k].astype(F32)
        qkv = (qkv * scale).astype(BF16)
        scores = dot_nt(qkv[:, 0:128], qkv[:, 128:256]) * HD ** (-0.5)
        seg_row = seg[2 * c + t % 2, pl.ds(t // 2, 1), :][:, 0:MB].astype(F32)
        allowed = (to_col(seg_row) == seg_row) & (iota((MB, MB), 1) <= iota((MB, MB), 0))
        scores = jnp.where(allowed, scores, -jnp.inf)
        weights = jnp.exp(scores - jnp.max(scores, axis=1, keepdims=True))
        probs = (weights / jnp.sum(weights, axis=1, keepdims=True)).astype(BF16)
        mx[t] = dot(probs, qkv[:, 256:384]).astype(BF16)
        place = mixed.at[t, 4 * odd + x]
        for dz in FAR:
            remote(
                mx.at[t], place, mx_s.at[1, t], mx_r.at[t], at(ring, y, (z + dz) % NZ, c)
            ).start()

        @pl.when(self_mx)
        def _():
            local(mx.at[t], place, mx_r.at[t]).start()

        @pl.when(jnp.logical_not(self_mx))
        def _():
            remote(mx.at[t], place, mx_s.at[0, t], mx_r.at[t], at(ring, y, z, c)).start()

    def back(t):
        settle(mixed.at[t], mx_r.at[t])
        whole = jnp.concatenate([mixed[t, j] for j in range(8)], axis=1)
        group = 2 * c + t % 2
        seg_row = seg[group, pl.ds(t // 2, 1), :][:, 0:MB]
        hits = seg_row == iota((16, MB), 0)
        amount = jnp.maximum(jnp.sum(hits.astype(F32), axis=1, keepdims=True), 1.0)
        for jj in range(2):
            sums = dot(whole, wo_v[jj])
            kept = hid[t, 2 * odd + jj].astype(F32)
            sums = (sums + jnp.where(x == ring, kept, 0.0)).astype(BF16)

            @pl.when(y < 3)
            def _():
                for i in range(2):
                    o_out[t, 2 * jj + i] = sums[:, 256 * i : 256 * i + 256]

            @pl.when(y == 3)
            def _():
                e_out[t, jj] = (dot(hits.astype(BF16), sums) / amount).astype(BF16)
                place = e_in.at[4 * x + group]
                for k in (2, 1, 3):
                    remote(
                        e_out.at[t, jj], place, e_s.at[1, t], e_r, at(turn(k), t // 2, z, jj)
                    ).start()
                is_self = (t // 2 == 3) & (c == jj)

                @pl.when(is_self)
                def _():
                    local(e_out.at[t, jj], place, e_r).start()

                @pl.when(jnp.logical_not(is_self))
                def _():
                    remote(
                        e_out.at[t, jj], place, e_s.at[0, t], e_r, at(x, t // 2, z, jj)
                    ).start()

        @pl.when(y < 3)
        def _():
            for k in (2, 1, 3):
                to = turn(k)
                remote(
                    o_out.at[t, to], o_in.at[t, k - 1], o_s.at[t], o_r.at[t], at(to, y, z, c)
                ).start()

    def forward(t):
        @pl.when(y < 3)
        def _():
            settle(o_in.at[t], o_r.at[t])
            new = o_out[t, x].astype(F32)
            for k in range(3):
                new = new + o_in[t, k].astype(F32)
            h_out[t] = new.astype(BF16)
            for dz in FAR + (0,):
                remote(
                    h_out.at[t], hid.at[t, 2 * odd + x // 2, :, half_of(x)], h_s.at[t], h_r.at[t],
                    at(ring, y + 1, (z + dz) % NZ, c),
                ).start()

    def ask(t):
        project(t)

        @pl.when((y == 0) & ((t == 0) | (t == 1) | (t == 3)))
        def _():
            pl.semaphore_signal(
                go, inc=1, device_id=at(x, (t + 3) // 2, z, c), device_id_type=MESH
            )

    stages = (ask, attend, back, forward)

    def word_of(k):
        word = jnp.int32(0)
        for plane, order in enumerate(ORDERS):
            for i in range(4 * T // 8):
                value = sum("PABF".index(s) * 4**n for n, s in enumerate(order[8 * i : 8 * i + 8]))
                word = jnp.where((y == plane) & (k // 8 == i), value, word)
        return word

    def tick(k, state):
        word, *counts = state
        word = jnp.where(k % 8 == 0, word_of(k), word)
        code = word % 4
        for s, stage in enumerate(stages):
            @pl.when(code == s)
            def _():
                stage(counts[s])
        counts = [n + jnp.where(code == s, 1, 0) for s, n in enumerate(counts)]
        return (word // 4, *counts)

    lax.fori_loop(0, 4 * T, tick, (jnp.int32(0),) * 5)

    settle(raw.at[0:3], x3_s.at[0])
    settle(seg.at[0:3], x3_s.at[1])
    settle(code.at[0:3], x3_s.at[2])
    settle(wq_v.at[0], one_s.at[0])
    settle(wo_v.at[0], one_s.at[1])
    for k in range(3):
        settle(kvt.at[0], kv_s.at[k])

    for h in range(2):
        @pl.when(y == 0)
        def _():
            settle(h_out.at[0:7], pro_s.at[1, h])

            @pl.when(jnp.logical_not(self_pro))
            def _():
                settle(packed.at[h], pro_s.at[0, h])

        @pl.when(y > 0)
        def _():
            settle(h_out, pro_s.at[1, h])

            @pl.when(jnp.logical_not(self_st))
            def _():
                settle(packed.at[h], st_s.at[h])

    def drain(t, carry):
        settle(q_in.at[t], q_s.at[t])
        settle(s_in.at[t], s_s.at[t])
        settle(mixed.at[t, 0:7], mx_s.at[1, t])

        @pl.when(jnp.logical_not(self_mx))
        def _():
            settle(mx.at[t], mx_s.at[0, t])

        @pl.when(y < 3)
        def _():
            settle(o_in.at[t], o_s.at[t])
            settle(hid.at[t], h_s.at[t])

        @pl.when(y == 3)
        def _():
            settle(e_in.at[0:6], e_s.at[1, t])

            @pl.when(t // 2 < 3)
            def _():
                settle(e_in.at[0:2], e_s.at[0, t])

            @pl.when(t // 2 == 3)
            def _():
                settle(e_in.at[0], e_s.at[0, t])

        return carry

    lax.fori_loop(0, T, drain, 0)

    settle(e_in, e_r)
    row = iota((16, 16), 0)
    col = iota((16, 16), 1)
    picked = jnp.zeros((16, BLK), F32)
    for g in range(NX):
        hits = ((row >> 1) & 3) == g
        hits = hits & ((row >= 8) == (col >= 3)) & (col < 6)
        hits = (hits & (code[g, 0:1, 0:16] == 2 * x + (row & 1))).astype(BF16)
        mean = e_in[g].astype(F32)
        for k in range(1, NX):
            mean = mean + e_in[4 * k + g].astype(F32)
        picked = picked + dot(hits, mean.astype(BF16))
    out[...] = picked.astype(BF16)


def shards(prompt_rows, row_dest, segment_ids, owner, gain, w_query, w_key, w_value, w_out):
    any_spec = pl.BlockSpec(memory_space=pl.ANY)
    vmem = pl.BlockSpec(memory_space=pltpu.VMEM)
    smem = pl.BlockSpec(memory_space=pltpu.SMEM)
    dma = pltpu.SemaphoreType.DMA
    embedded = pl.pallas_call(
        kernel,
        out_shape=jax.ShapeDtypeStruct((16, BLK), BF16),
        in_specs=[any_spec, vmem, vmem, smem, vmem, any_spec, any_spec, any_spec, any_spec],
        out_specs=vmem,
        scratch_shapes=[
            pltpu.VMEM((NX, MB, 256), BF16),
            pltpu.VMEM((NX, 8, 128), I32),
            pltpu.VMEM((NX, 8, 128), I32),
            pltpu.VMEM((2, 2048, 256), BF16),
            pltpu.VMEM((4, 2, 32, 2048), BF16),
            pltpu.VMEM((2048, 256), BF16),
            pltpu.VMEM((2, 1024, BLK), BF16),
            pltpu.VMEM((2, MB, 256), BF16),
            pltpu.VMEM((2, MB, 256), BF16),
            pltpu.VMEM((T, 4, MB, BLK), BF16),
            pltpu.VMEM((T, 4, MB, 384), BF16),
            pltpu.VMEM((T, 3, MB, 384), BF16),
            pltpu.VMEM((T, 8, 128), F32),
            pltpu.VMEM((T, 3, 8, 128), F32),
            pltpu.VMEM((T, MB, 128), BF16),
            pltpu.VMEM((T, 8, MB, 128), BF16),
            pltpu.VMEM((T, 4, MB, 256), BF16),
            pltpu.VMEM((T, 3, MB, 256), BF16),
            pltpu.VMEM((T, MB, 256), BF16),
            pltpu.VMEM((T, 2, 16, BLK), BF16),
            pltpu.VMEM((4 * NX, 16, BLK), BF16),
            dma((5,)),
            dma((2,)),
            dma((2,)),
            dma((3,)),
            dma((3,)),
            dma((3,)),
            dma((3,)),
            dma((2, 2)),
            dma((T,)),
            dma((T,)),
            dma((T,)),
            dma((T,)),
            dma((T,)),
            dma((2, T)),
            dma((T,)),
            dma((T,)),
            dma((T,)),
            dma((T,)),
            dma((2, T)),
            dma,
            pltpu.SemaphoreType.REGULAR,
            dma((2,)),
            dma,
        ],
        compiler_params=pltpu.CompilerParams(
            collective_id=0, has_side_effects=True, vmem_limit_bytes=60 << 20
        ),
        name="sections",
    )(
        prompt_rows.reshape(MB, BLK),
        row_dest,
        segment_ids,
        owner.reshape(2, 3),
        gain,
        w_query[0],
        w_key[0].T,
        w_value[0].T,
        w_out[0],
    )
    return embedded.reshape(1, 2, 8, BLK)


def solution(mesh):
    in_specs = (
        P("dp", "phase", None, "mp"),
        P(None, "phase", None),
        P("dp", None, None),
        P("dp", "phase", None, None),
        P("phase", None),
        P("phase", "dp", "mp"),
        P("phase", "dp", "mp"),
        P("phase", "dp", "mp"),
        P("phase", "dp", "mp"),
    )
    out_specs = P("dp", "phase", None, "mp")
    return jax.shard_map(shards, mesh=mesh, in_specs=in_specs, out_specs=out_specs, check_vma=False)
```
